512 devices in a mesh: group: 32 (over x, z), section: 2 (over core), tensor: 8 (over y).
Axes of the slice: x: 4, y: 8, z: 8, core: 2. Of those that a mesh axis runs over, the one named last changes fastest.
Arguments:
- queries: bfloat16 [2, 64, 4096], P('section', 'group', 'tensor'), may hold values from -100 to 100, as said below
- kv_cache: bfloat16 [2, 64, 2, 512, 1024], P('section', 'group', None, None, 'tensor'), may hold values from -20 to 20, as said below
- new_kv: bfloat16 [2, 64, 2, 1024], P('section', 'group', None, 'tensor'), may hold values from -6 to 6
- residual: bfloat16 [2, 64, 4096], P('section', 'group', 'tensor'), may hold values from -6 to 6
- out_weight: bfloat16 [2, 4096, 4096], P('section', 'tensor'), may hold values from -0.5 to 0.5
- dest_cell: int32 [64], replicated, may hold values from 0 to 127, as said below
- lengths: int32 [64], replicated, may hold values from 1 to 511
Outputs:
- handed: bfloat16 [2, 128, 4096], P('section', 'group', 'tensor')
- migrated_cache: bfloat16 [2, 128, 2, 512, 1024], P('section', 'group', None, None, 'tensor')
The draws below stay inside these ranges and needn't reach their ends.
Inputs may be any that keep to these rules, and one draw needn't show every extreme that they name: queries lie within the stated bounds. `kv_cache`: cache entries lie within the stated bounds. `dest_cell`: entries are distinct; dest_cell[r] // 4 is the group that row r moves to, and rows r with the same r // 2 start in the same group. Half of the groups receive exactly 4 rows each, the others none; the rows of one group go to distinct groups.
All inputs are finite; a program needn't handle non-finite values.
Results may differ from the reference program's by a relative error of at most 0.008.
Values may be sent and summed in bfloat16 or wider, within the bound.
A program may use at most 64 MiB of HBM per device.

```python
import jax
import jax.numpy as jnp

HD = 128
KVH = 8
QH = 32
DW = 4096
CTX = 512
R_DEV = 2
CAP = 4
ROWS = 64
CELLS = 128
LAYERS = 2
N_GROUP = 32


def draw_queries(key, part):
    key = jax.random.fold_in(key, 12)
    noise_key = jax.random.fold_in(key, 0)
    values = jax.random.truncated_normal(noise_key, -6.0, 6.0, (LAYERS, ROWS, QH * HD), jnp.float32)
    return values.astype(jnp.bfloat16)


def draw_kv_cache(key, part):
    key = jax.random.fold_in(key, 11)
    full_shape = (LAYERS, ROWS, 2, CTX, KVH * HD)
    values = jax.random.truncated_normal(key, -6.0, 6.0, full_shape, jnp.float32)
    return values.astype(jnp.bfloat16)


def draw_dest_cell(key, part):
    key = jax.random.fold_in(key, 5)
    rank_key, spare_key = jax.random.split(key)
    half_groups = N_GROUP // 2
    source_rank = jax.random.permutation(rank_key, N_GROUP).astype(jnp.int32)
    spare_base = jax.random.permutation(spare_key, N_GROUP).astype(jnp.int32)
    spare_order = (spare_base + (N_GROUP - 1) - spare_base[0]) % N_GROUP
    row_ids = jnp.arange(ROWS, dtype=jnp.int32)
    source_group = row_ids // R_DEV
    local_index = row_ids % R_DEV
    rank_value = source_rank[source_group]
    target_index = (rank_value // 2 + local_index) % half_groups
    target_group = spare_order[target_index]
    slot_value = local_index * 2 + rank_value % 2
    return (target_group * CAP + slot_value).astype(jnp.int32)


def place_ends(result, own_key, least, top_value):
    shape = result.shape
    spot = [jax.random.randint(jax.random.fold_in(own_key, axis), (), 0, shape[axis]) for axis in range(len(shape))]
    result = result.at[tuple(spot)].set(least)
    longest = shape.index(max(shape))
    spot[longest] = (spot[longest] + 1) % shape[longest]
    return result.at[tuple(spot)].set(top_value)


def shard_levels(stream_key, extent, shards, least, top_value):
    loudness = 1.0
    for position, shards_of in shards:
        steps = jax.random.uniform(jax.random.fold_in(jax.random.fold_in(stream_key, 6), position), (shards_of,), jnp.float32, least / len(shards), top_value / len(shards))
        loudness = loudness * jnp.repeat(jnp.exp(steps), extent[position] // shards_of).reshape((-1,) + (1,) * (len(extent) - 1 - position))
    return loudness


def noise(stream_key, shape, spread, most, cuts=(), kind=jnp.bfloat16):
    loudness = shard_levels(stream_key, shape, cuts, -0.22, 0.18) if cuts else 1.0
    entries = jax.random.normal(stream_key, shape, jnp.float32) * spread * loudness
    return jnp.minimum(jnp.maximum(entries, -most), most).astype(kind)


def setup_inputs(seed: int = 0) -> dict:
    seeds = jax.random.split(jax.random.key(seed), 8)
    return {
        "queries": draw_queries(jax.random.fold_in(seeds[7], 71), 0),
        "kv_cache": draw_kv_cache(jax.random.fold_in(seeds[7], 71), 0),
        "new_kv": noise(seeds[2], (LAYERS, ROWS, 2, KVH * HD), 1.0, 6.0, ((0, 2), (1, 32), (3, 8))),
        "residual": noise(seeds[3], (LAYERS, ROWS, DW), 1.0, 6.0, ((0, 2), (1, 32), (2, 8))),
        "out_weight": noise(seeds[4], (LAYERS, QH * HD, DW), HD ** -0.5, 0.5, ((0, 2), (1, 8))),
        "dest_cell": draw_dest_cell(jax.random.fold_in(seeds[7], 71), 0),
        "lengths": place_ends(jax.random.randint(seeds[6], (ROWS,), 1, CTX), jax.random.fold_in(seeds[6], 1), 1, CTX - 1).astype(jnp.int32),
    }


NEG_FILL = -1.0e30


def attend(query_rows, cache_rows, fresh_rows, valid_counts, kv_heads):
    n_rows = query_rows.shape[0]
    positions = cache_rows.shape[2]
    head_dim = fresh_rows.shape[-1] // kv_heads
    group_ratio = query_rows.shape[-1] // (kv_heads * head_dim)
    score_scale = 1.0 / (head_dim ** 0.5)
    query_heads = query_rows.astype(jnp.float32).reshape(n_rows, kv_heads, group_ratio, head_dim)
    keys_all = cache_rows[:, 0].astype(jnp.float32).reshape(n_rows, positions, kv_heads, head_dim)
    values_all = cache_rows[:, 1].astype(jnp.float32).reshape(n_rows, positions, kv_heads, head_dim)
    fresh_key = fresh_rows[:, 0].astype(jnp.float32).reshape(n_rows, kv_heads, head_dim)
    fresh_value = fresh_rows[:, 1].astype(jnp.float32).reshape(n_rows, kv_heads, head_dim)
    scores = jnp.einsum('ngrd,npgd->ngrp', query_heads, keys_all) * score_scale
    own_score = jnp.einsum('ngrd,ngd->ngr', query_heads, fresh_key) * score_scale
    valid = (jnp.arange(positions, dtype=jnp.int32)[None, :] < valid_counts[:, None])[:, None, None, :]
    masked = jnp.where(valid, scores, NEG_FILL)
    row_top = jnp.maximum(jnp.max(masked, axis=-1), own_score)
    exp_scores = jnp.where(valid, jnp.exp(masked - row_top[..., None]), 0.0)
    own_exp = jnp.exp(own_score - row_top)
    denominator = jnp.sum(exp_scores, axis=-1) + own_exp
    weights = (exp_scores / denominator[..., None]).astype(jnp.bfloat16)
    own_weight = (own_exp / denominator).astype(jnp.bfloat16)
    mixed = jnp.einsum('ngrp,npgd->ngrd', weights.astype(jnp.float32), values_all)
    mixed = mixed + own_weight.astype(jnp.float32)[..., None] * fresh_value[:, :, None, :]
    return mixed.reshape(n_rows, -1).astype(jnp.bfloat16)


def append_token(cache_rows, fresh_rows, valid_counts):
    positions = cache_rows.shape[2]
    at_end = jnp.arange(positions, dtype=jnp.int32)[None, :] == valid_counts[:, None]
    return jnp.where(at_end[:, None, :, None], fresh_rows[:, :, None, :], cache_rows)


def reference(queries, kv_cache, new_kv, residual, out_weight, dest_cell, lengths):
    outputs = []
    caches = []
    for section_layer in range(LAYERS):
        attended = attend(queries[section_layer], kv_cache[section_layer], new_kv[section_layer], lengths, KVH)
        projected = jnp.dot(attended, out_weight[section_layer], preferred_element_type=jnp.float32)
        rows_out = (residual[section_layer].astype(jnp.float32) + projected).astype(jnp.bfloat16)
        placed = jnp.zeros((CELLS, DW), jnp.bfloat16).at[dest_cell].set(rows_out)
        outputs.append(placed)
        extended = append_token(kv_cache[section_layer], new_kv[section_layer], lengths)
        moved = jnp.zeros((CELLS, 2, CTX, KVH * HD), jnp.bfloat16).at[dest_cell].set(extended)
        caches.append(moved)
    stacked = jnp.stack(outputs)
    return jnp.roll(stacked, 1, axis=0), jnp.stack(caches)
```

```python
import functools

import jax
import jax.numpy as jnp
from jax import lax
from jax.experimental import pallas as pl
from jax.experimental.pallas import tpu as pltpu
from jax.sharding import PartitionSpec as P

HD = 128
NZ = 8
MESH = pl.DeviceIdType.MESH


def move_kernel(
    nx, nz, nt,
    dest_hbm, len_hbm, q_hbm, kv_hbm, fresh_hbm, res_hbm, w_hbm,
    handed_ref, cache_ref,
    dest_ref, len_ref, q_ref, fresh_ref, res_ref, row_of, row_of_ref,
    kv, w, got_k, got_v, put_k, put_v, part, red, lay_own, lay,
    in_sem, small_sem, row_sem, w_sem, own_sem, sent_sem, k1_sem, v1_sem, k2_sem, v2_sem, red_sent, red_sem, layz_sent, layx_sent, layz_sem, layx_sem,
):
    groups = nx * nz
    ctx = kv.shape[2]
    span = ctx // groups
    rows = 2 * groups
    g = lax.axis_index("group")
    s = lax.axis_index("section")
    t = lax.axis_index("tensor")
    x = g // nz
    z = g % nz

    load_kv = pltpu.make_async_copy(kv_hbm.at[0], kv, in_sem)
    load_kv.start()
    small = [
        pltpu.make_async_copy(src, dst, small_sem.at[i])
        for i, (src, dst) in enumerate(
            ((len_hbm, len_ref), (fresh_hbm, fresh_ref), (q_hbm, q_ref), (dest_hbm, dest_ref), (res_hbm, res_ref))
        )
    ]
    for load in small:
        load.start()

    barrier = pltpu.get_barrier_semaphore()

    def greet_group(k, carry):
        pl.semaphore_signal(barrier, inc=1, device_id={"group": (g + k) % groups}, device_id_type=MESH)
        return carry

    def greet_tensor(k, carry):
        pl.semaphore_signal(barrier, inc=1, device_id={"tensor": (t + k) % nt}, device_id_type=MESH)
        return carry

    def greet_section(k, carry):
        pl.semaphore_signal(
            barrier, inc=1, device_id={"group": x * nz + (z + k) % nz, "section": 1 - s}, device_id_type=MESH
        )
        return carry

    lax.fori_loop(1, groups, greet_group, 0)
    lax.fori_loop(1, nt, greet_tensor, 0)
    lax.fori_loop(0, nz, greet_section, 0)

    for load in small:
        load.wait()
    len0 = len_ref[2 * g]
    len1 = len_ref[2 * g + 1]
    load_kv.wait()
    load_w = pltpu.make_async_copy(w_hbm.at[0], w, w_sem)
    load_w.start()
    pos = lax.broadcasted_iota(jnp.int32, (ctx, HD), 0)
    for r, n in ((0, len0), (1, len1)):
        here = pos == n
        for c in range(2):
            token = jnp.broadcast_to(fresh_ref[0, r, c : c + 1, :].astype(jnp.float32), (ctx, HD))
            kv[r, c] = jnp.where(here, token, kv[r, c].astype(jnp.float32)).astype(jnp.bfloat16)
    zero = jnp.zeros((span, HD), jnp.bfloat16)
    got_k[rows] = zero
    got_v[rows] = zero
    mine = pl.ds(pl.multiple_of(span * g, span), span)
    for r in range(2):
        got_k[2 * g + r] = kv[r, 0, mine, :]
        got_v[2 * g + r] = kv[r, 1, mine, :]

    pl.semaphore_wait(barrier, groups - 1 + nt - 1 + nz)

    def partner(k):
        i = k + jnp.where(k >= 1, 1, 0)
        far = nz // 2 - i // (2 * nx)
        dx = (i // 2) % nx
        dz = jnp.where(i % 2 == 0, far, jnp.where(far == nz // 2, 0, nz - far))
        return ((x + dx) % nx) * nz + (z + dz) % nz

    def hop1(c, dst, sem):
        def send(k, carry):
            d = partner(k)
            pltpu.make_async_remote_copy(
                src_ref=kv.at[:, c, pl.ds(pl.multiple_of(span * d, span), span), :],
                dst_ref=dst.at[pl.ds(2 * g, 2)],
                send_sem=sent_sem.at[c],
                recv_sem=sem,
                device_id={"group": d},
                device_id_type=MESH,
            ).start()
            return carry

        lax.fori_loop(0, groups - 1, send, 0)

    hop1(0, got_k, k1_sem)
    hop1(1, got_v, v1_sem)

    cells = row_of.shape[1]
    cell = lax.broadcasted_iota(jnp.int32, (8, cells), 1)

    def place(r, found):
        return jnp.where(cell == dest_ref[r], r, found)

    found = lax.fori_loop(0, rows, place, jnp.full((8, cells), rows, jnp.int32), unroll=8)
    row_of[...] = found
    load_row_of = pltpu.make_async_copy(row_of, row_of_ref, row_sem)
    load_row_of.start()

    qf = q_ref[0].astype(jnp.float32)
    q8 = jnp.concatenate(
        [qf[r : r + 1, h * HD : (h + 1) * HD] for r in range(2) for h in range(4)], axis=0
    ).astype(jnp.bfloat16)
    dims = (((1,), (1,)), ((), ()))
    first = lax.broadcasted_iota(jnp.int32, (8, ctx), 0) < 4
    scores = jnp.where(
        first,
        lax.dot_general(q8, kv[0, 0], dims, preferred_element_type=jnp.float32),
        lax.dot_general(q8, kv[1, 0], dims, preferred_element_type=jnp.float32),
    ) * (1.0 / HD**0.5)
    valid = lax.broadcasted_iota(jnp.int32, (8, ctx), 1) <= jnp.where(first, len0, len1)
    scores = jnp.where(valid, scores, -1e30)
    top = jnp.max(scores, axis=1, keepdims=True)
    e = jnp.where(valid, jnp.exp(scores - top), 0.0)
    weights = (e / jnp.sum(e, axis=1, keepdims=True)).astype(jnp.bfloat16)
    sub = lax.broadcasted_iota(jnp.int32, (8, HD), 0)
    attended = jnp.where(
        sub < 4,
        jnp.dot(weights, kv[0, 1], preferred_element_type=jnp.float32),
        jnp.dot(weights, kv[1, 1], preferred_element_type=jnp.float32),
    )
    lhs = jnp.concatenate(
        [jnp.where(sub % 4 == h, attended, 0.0) for h in range(4)], axis=1
    ).astype(jnp.bfloat16)

    def wait_bytes(ref, sem):
        pltpu.make_async_copy(ref, ref, sem).wait()

    def hop2(c, got, put, sem, own):
        def copy_slots(d):
            for slot in range(4):
                put[4 * d + slot] = got[row_of_ref[0, 4 * d + slot]]

        def send(k, carry):
            d = partner(k)
            copy_slots(d)
            pltpu.make_async_remote_copy(
                src_ref=put.at[pl.ds(4 * d, 4)],
                dst_ref=cache_ref.at[0, :, c, mine, :],
                send_sem=sent_sem.at[2 + c],
                recv_sem=sem,
                device_id={"group": d},
                device_id_type=MESH,
            ).start()
            return carry

        lax.fori_loop(0, groups - 1, send, 0)
        copy_slots(g)
        pltpu.make_async_copy(put.at[pl.ds(4 * g, 4)], cache_ref.at[0, :, c, mine, :], own).start()

    load_row_of.wait()
    wait_bytes(got_k.at[pl.ds(0, rows - 2)], k1_sem)
    hop2(0, got_k, put_k, k2_sem, own_sem.at[0])

    width = res_ref.shape[2]
    load_w.wait()

    def project(k, carry):
        d = (t + k) % nt
        cols = pl.ds(pl.multiple_of(width * d, width), width)
        p8 = jnp.dot(lhs, w[:, cols], preferred_element_type=jnp.float32)
        both = jnp.concatenate(
            [jnp.sum(p8[0:4], axis=0, keepdims=True), jnp.sum(p8[4:8], axis=0, keepdims=True)], axis=0
        )
        part[d] = both

        @pl.when(k < nt)
        def _():
            pltpu.make_async_remote_copy(
                src_ref=part.at[d],
                dst_ref=red.at[t],
                send_sem=red_sent,
                recv_sem=red_sem,
                device_id={"tensor": d},
                device_id_type=MESH,
            ).start()

        return carry

    lax.fori_loop(1, nt + 1, project, 0)
    red[t] = part[t]

    wait_bytes(got_v.at[pl.ds(0, rows - 2)], v1_sem)
    hop2(1, got_v, put_v, v2_sem, own_sem.at[1])

    wait_bytes(red.at[pl.ds(0, nt - 1)], red_sem)
    total = red[0]
    for i in range(1, nt):
        total = total + red[i]
    total = total + res_ref[0].astype(jnp.float32)
    lay_own[0] = total[0:1]
    lay_own[1] = total[1:2]

    def hand(k, carry):
        pltpu.make_async_remote_copy(
            src_ref=lay_own,
            dst_ref=lay.at[pl.ds(2 * g, 2)],
            send_sem=layz_sent,
            recv_sem=layz_sem,
            device_id={"group": x * nz + (z + k) % nz, "section": 1 - s},
            device_id_type=MESH,
        ).start()
        return carry

    lax.fori_loop(0, nz, hand, 0)

    ring = pl.ds(2 * nz * x, 2 * nz)
    wait_bytes(lay.at[pl.ds(0, 2 * nz)], layz_sem)

    def spread(k, carry):
        pltpu.make_async_remote_copy(
            src_ref=lay.at[ring],
            dst_ref=lay.at[ring],
            send_sem=layx_sent,
            recv_sem=layx_sem,
            device_id={"group": ((x + k) % nx) * nz + z},
            device_id_type=MESH,
        ).start()
        return carry

    lax.fori_loop(1, nx, spread, 0)
    wait_bytes(lay.at[pl.ds(0, 2 * nz * (nx - 1))], layx_sem)
    out_rows = []
    for slot in range(4):
        r = row_of_ref[0, 4 * g + slot]
        out_rows.append(jnp.where(r < rows, lay[jnp.minimum(r, rows - 1)], 0.0))
    handed_ref[0] = jnp.concatenate(out_rows, axis=0).astype(jnp.bfloat16)

    wait_bytes(part.at[pl.ds(0, nt - 1)], red_sent)
    wait_bytes(lay.at[pl.ds(0, 2 * nz)], layz_sent)
    wait_bytes(lay.at[pl.ds(0, 2 * nz * (nx - 1))], layx_sent)
    wait_bytes(got_k.at[pl.ds(0, rows - 2)], sent_sem.at[0])
    wait_bytes(got_v.at[pl.ds(0, rows - 2)], sent_sem.at[1])
    for c, put, sem in ((0, put_k, k2_sem), (1, put_v, v2_sem)):
        pltpu.make_async_copy(put.at[pl.ds(4 * g, 4)], cache_ref.at[0, :, c, mine, :], own_sem.at[c]).wait()
        wait_bytes(put.at[pl.ds(0, 4 * (groups - 1))], sent_sem.at[2 + c])
        wait_bytes(put.at[pl.ds(0, 4 * (groups - 1))], sem)


def write_kernel(handed, moved, handed_hbm, moved_hbm, sem):
    copies = [pltpu.make_async_copy(moved.at[0, i], moved_hbm.at[0, i], sem.at[i]) for i in range(4)]
    copies.append(pltpu.make_async_copy(handed, handed_hbm, sem.at[4]))
    for copy in copies:
        copy.start()
    for copy in copies:
        copy.wait()


def shards(nx, nz, nt, queries, kv_cache, new_kv, residual, out_weight, dest_cell, lengths):
    groups = nx * nz
    rows = 2 * groups
    cells = 4 * groups
    ctx = kv_cache.shape[3]
    span = ctx // groups
    width = residual.shape[-1]
    bf = jnp.bfloat16
    f32 = jnp.float32
    dma = pltpu.SemaphoreType.DMA
    vmem = pl.BlockSpec(memory_space=pltpu.VMEM)
    hbm = pl.BlockSpec(memory_space=pltpu.HBM)
    handed, moved = pl.pallas_call(
        functools.partial(move_kernel, nx, nz, nt),
        out_shape=(pltpu.VMEM((1, 4, width), bf), pltpu.VMEM((1, 4, 2, ctx, HD), bf)),
        in_specs=[hbm] * 7,
        out_specs=(vmem, vmem),
        scratch_shapes=[
            pltpu.SMEM((rows,), jnp.int32),
            pltpu.SMEM((rows,), jnp.int32),
            pltpu.VMEM(queries.shape, bf),
            pltpu.VMEM(new_kv.shape, bf),
            pltpu.VMEM(residual.shape, bf),
            pltpu.VMEM((8, cells), jnp.int32),
            pltpu.SMEM((8, cells), jnp.int32),
            pltpu.VMEM((2, 2, ctx, HD), bf),
            pltpu.VMEM(out_weight.shape[1:], bf),
            pltpu.VMEM((rows + 1, span, HD), bf),
            pltpu.VMEM((rows + 1, span, HD), bf),
            pltpu.VMEM((cells, span, HD), bf),
            pltpu.VMEM((cells, span, HD), bf),
            pltpu.VMEM((nt, 2, width), f32),
            pltpu.VMEM((nt, 2, width), f32),
            pltpu.VMEM((2, 1, width), f32),
            pltpu.VMEM((rows, 1, width), f32),
            dma, dma((5,)), dma, dma, dma((2,)), dma((4,)), dma, dma, dma, dma, dma, dma, dma, dma, dma, dma,
        ],
        compiler_params=pltpu.CompilerParams(
            collective_id=0, has_side_effects=True, vmem_limit_bytes=60 * 1024 * 1024
        ),
    )(dest_cell, lengths, queries, kv_cache, new_kv, residual, out_weight)
    return pl.pallas_call(
        write_kernel,
        out_shape=(
            jax.ShapeDtypeStruct(handed.shape, bf),
            jax.ShapeDtypeStruct(moved.shape, bf),
        ),
        in_specs=[vmem, vmem],
        out_specs=(hbm, hbm),
        scratch_shapes=[dma((5,))],
    )(handed, moved)


def solution(mesh):
    in_specs = (
        P("section", "group", "tensor"),
        P("section", "group", None, None, "tensor"),
        P("section", "group", None, "tensor"),
        P("section", "group", "tensor"),
        P("section", "tensor", None),
        P(),
        P(),
    )
    out_specs = (P("section", "group", "tensor"), P("section", "group", None, None, "tensor"))
    nz = min(NZ, mesh.shape["group"] // 2)
    body = functools.partial(shards, mesh.shape["group"] // nz, nz, mesh.shape["tensor"])
    return jax.shard_map(body, mesh=mesh, in_specs=in_specs, out_specs=out_specs, check_vma=False)
```

```python
import functools

import jax
import jax.numpy as jnp
from jax import lax
from jax.experimental import pallas as pl
from jax.experimental.pallas import tpu as pltpu
from jax.sharding import PartitionSpec as P

HD = 128
NZ = 8
MESH = pl.DeviceIdType.MESH


def move_kernel(
    nx, nz, nt,
    dest_hbm, len_hbm, q_hbm, kv_hbm, fresh_hbm, res_hbm, w_hbm,
    handed_ref, cache_ref,
    dest_ref, len_ref, q_ref, fresh_ref, res_ref, row_of, row_of_ref,
    kv, w, got_k, got_v, put_k, put_v, part, red, lay_own, lay,
    in_sem, small_sem, row_sem, w_sem, own_sem, sent_sem, k1_sem, v1_sem, k2_sem, v2_sem, red_sent, red_sem, layz_sent, layx_sent, layz_sem, layx_sem,
):
    groups = nx * nz
    ctx = kv.shape[2]
    span = ctx // groups
    rows = 2 * groups
    g = lax.axis_index("group")
    s = lax.axis_index("section")
    t = lax.axis_index("tensor")
    x = g // nz
    z = g % nz

    load_kv = pltpu.make_async_copy(kv_hbm.at[0], kv, in_sem)
    load_kv.start()
    small = [
        pltpu.make_async_copy(src, dst, small_sem.at[i])
        for i, (src, dst) in enumerate(
            ((len_hbm, len_ref), (fresh_hbm, fresh_ref), (q_hbm, q_ref), (dest_hbm, dest_ref), (res_hbm, res_ref))
        )
    ]
    for load in small:
        load.start()

    barrier = pltpu.get_barrier_semaphore()

    def greet_group(k, carry):
        pl.semaphore_signal(barrier, inc=1, device_id={"group": (g + k) % groups}, device_id_type=MESH)
        return carry

    def greet_tensor(k, carry):
        pl.semaphore_signal(barrier, inc=1, device_id={"tensor": (t + k) % nt}, device_id_type=MESH)
        return carry

    def greet_section(k, carry):
        pl.semaphore_signal(
            barrier, inc=1, device_id={"group": x * nz + (z + k) % nz, "section": 1 - s}, device_id_type=MESH
        )
        return carry

    lax.fori_loop(1, groups, greet_group, 0)
    lax.fori_loop(1, nt, greet_tensor, 0)
    lax.fori_loop(0, nz, greet_section, 0)

    for load in small:
        load.wait()
    len0 = len_ref[2 * g]
    len1 = len_ref[2 * g + 1]
    load_kv.wait()
    load_w = pltpu.make_async_copy(w_hbm.at[0], w, w_sem)
    load_w.start()
    pos = lax.broadcasted_iota(jnp.int32, (ctx, HD), 0)
    for r, n in ((0, len0), (1, len1)):
        here = pos == n
        for c in range(2):
            token = jnp.broadcast_to(fresh_ref[0, r, c : c + 1, :].astype(jnp.float32), (ctx, HD))
            kv[r, c] = jnp.where(here, token, kv[r, c].astype(jnp.float32)).astype(jnp.bfloat16)
    zero = jnp.zeros((span, HD), jnp.bfloat16)
    got_k[rows] = zero
    got_v[rows] = zero
    mine = pl.ds(pl.multiple_of(span * g, span), span)
    for r in range(2):
        got_k[2 * g + r] = kv[r, 0, mine, :]
        got_v[2 * g + r] = kv[r, 1, mine, :]

    pl.semaphore_wait(barrier, groups - 1 + nt - 1 + nz)

    def partner(k):
        i = k + jnp.where(k >= 1, 1, 0)
        far = nz // 2 - i // (2 * nx)
        dx = (i // 2) % nx
        dz = jnp.where(i % 2 == 0, far, jnp.where(far == nz // 2, 0, nz - far))
        return ((x + dx) % nx) * nz + (z + dz) % nz

    def hop1(c, dst, sem, low, high):
        def send(k, carry):
            d = partner(k)
            pltpu.make_async_remote_copy(
                src_ref=kv.at[:, c, pl.ds(pl.multiple_of(span * d, span), span), :],
                dst_ref=dst.at[pl.ds(2 * g, 2)],
                send_sem=sent_sem.at[c],
                recv_sem=sem,
                device_id={"group": d},
                device_id_type=MESH,
            ).start()
            return carry

        lax.fori_loop(low, high, send, 0)

    hop1(0, got_k, k1_sem, 0, groups - 1)

    cells = row_of.shape[1]
    cell = lax.broadcasted_iota(jnp.int32, (8, cells), 1)

    def place(r, found):
        return jnp.where(cell == dest_ref[r], r, found)

    found = lax.fori_loop(0, rows, place, jnp.full((8, cells), rows, jnp.int32), unroll=8)
    row_of[...] = found
    load_row_of = pltpu.make_async_copy(row_of, row_of_ref, row_sem)
    load_row_of.start()

    qf = q_ref[0].astype(jnp.float32)
    q8 = jnp.concatenate(
        [qf[r : r + 1, h * HD : (h + 1) * HD] for r in range(2) for h in range(4)], axis=0
    ).astype(jnp.bfloat16)
    dims = (((1,), (1,)), ((), ()))
    first = lax.broadcasted_iota(jnp.int32, (8, ctx), 0) < 4
    scores = jnp.where(
        first,
        lax.dot_general(q8, kv[0, 0], dims, preferred_element_type=jnp.float32),
        lax.dot_general(q8, kv[1, 0], dims, preferred_element_type=jnp.float32),
    ) * (1.0 / HD**0.5)
    valid = lax.broadcasted_iota(jnp.int32, (8, ctx), 1) <= jnp.where(first, len0, len1)
    scores = jnp.where(valid, scores, -1e30)
    top = jnp.max(scores, axis=1, keepdims=True)
    e = jnp.where(valid, jnp.exp(scores - top), 0.0)
    weights = (e / jnp.sum(e, axis=1, keepdims=True)).astype(jnp.bfloat16)
    sub = lax.broadcasted_iota(jnp.int32, (8, HD), 0)
    attended = jnp.where(
        sub < 4,
        jnp.dot(weights, kv[0, 1], preferred_element_type=jnp.float32),
        jnp.dot(weights, kv[1, 1], preferred_element_type=jnp.float32),
    )
    lhs = jnp.concatenate(
        [jnp.where(sub % 4 == h, attended, 0.0) for h in range(4)], axis=1
    ).astype(jnp.bfloat16)

    def wait_bytes(ref, sem):
        pltpu.make_async_copy(ref, ref, sem).wait()

    def hop2(c, got, put, sem, own):
        def copy_slots(d):
            for slot in range(4):
                put[4 * d + slot] = got[row_of_ref[0, 4 * d + slot]]

        def send(k, carry):
            d = partner(k)
            copy_slots(d)
            pltpu.make_async_remote_copy(
                src_ref=put.at[pl.ds(4 * d, 4)],
                dst_ref=cache_ref.at[0, :, c, mine, :],
                send_sem=sent_sem.at[2 + c],
                recv_sem=sem,
                device_id={"group": d},
                device_id_type=MESH,
            ).start()
            return carry

        lax.fori_loop(0, groups - 1, send, 0)
        copy_slots(g)
        pltpu.make_async_copy(put.at[pl.ds(4 * g, 4)], cache_ref.at[0, :, c, mine, :], own).start()

    hop1(1, got_v, v1_sem, 0, groups // 2)

    width = res_ref.shape[2]
    load_w.wait()

    def project(k, carry):
        d = (t + k) % nt
        cols = pl.ds(pl.multiple_of(width * d, width), width)
        p8 = jnp.dot(lhs, w[:, cols], preferred_element_type=jnp.float32)
        both = jnp.concatenate(
            [jnp.sum(p8[0:4], axis=0, keepdims=True), jnp.sum(p8[4:8], axis=0, keepdims=True)], axis=0
        )
        part[d] = both

        @pl.when(k < nt)
        def _():
            pltpu.make_async_remote_copy(
                src_ref=part.at[d],
                dst_ref=red.at[t],
                send_sem=red_sent,
                recv_sem=red_sem,
                device_id={"tensor": d},
                device_id_type=MESH,
            ).start()

        return carry

    lax.fori_loop(1, nt + 1, project, 0)
    red[t] = part[t]

    hop1(1, got_v, v1_sem, groups // 2, groups - 1)

    wait_bytes(red.at[pl.ds(0, nt - 1)], red_sem)
    total = red[0]
    for i in range(1, nt):
        total = total + red[i]
    total = total + res_ref[0].astype(jnp.float32)
    lay_own[0] = total[0:1]
    lay_own[1] = total[1:2]

    def hand(k, carry):
        pltpu.make_async_remote_copy(
            src_ref=lay_own,
            dst_ref=lay.at[pl.ds(2 * g, 2)],
            send_sem=layz_sent,
            recv_sem=layz_sem,
            device_id={"group": x * nz + (z + k) % nz, "section": 1 - s},
            device_id_type=MESH,
        ).start()
        return carry

    lax.fori_loop(0, nz, hand, 0)

    load_row_of.wait()
    wait_bytes(got_k.at[pl.ds(0, rows - 2)], k1_sem)
    hop2(0, got_k, put_k, k2_sem, own_sem.at[0])

    ring = pl.ds(2 * nz * x, 2 * nz)
    wait_bytes(lay.at[pl.ds(0, 2 * nz)], layz_sem)

    def spread(k, carry):
        pltpu.make_async_remote_copy(
            src_ref=lay.at[ring],
            dst_ref=lay.at[ring],
            send_sem=layx_sent,
            recv_sem=layx_sem,
            device_id={"group": ((x + k) % nx) * nz + z},
            device_id_type=MESH,
        ).start()
        return carry

    lax.fori_loop(1, nx, spread, 0)

    wait_bytes(got_v.at[pl.ds(0, rows - 2)], v1_sem)
    hop2(1, got_v, put_v, v2_sem, own_sem.at[1])

    wait_bytes(lay.at[pl.ds(0, 2 * nz * (nx - 1))], layx_sem)
    out_rows = []
    for slot in range(4):
        r = row_of_ref[0, 4 * g + slot]
        out_rows.append(jnp.where(r < rows, lay[jnp.minimum(r, rows - 1)], 0.0))
    handed_ref[0] = jnp.concatenate(out_rows, axis=0).astype(jnp.bfloat16)

    wait_bytes(part.at[pl.ds(0, nt - 1)], red_sent)
    wait_bytes(lay.at[pl.ds(0, 2 * nz)], layz_sent)
    wait_bytes(lay.at[pl.ds(0, 2 * nz * (nx - 1))], layx_sent)
    wait_bytes(got_k.at[pl.ds(0, rows - 2)], sent_sem.at[0])
    wait_bytes(got_v.at[pl.ds(0, rows - 2)], sent_sem.at[1])
    for c, put, sem in ((0, put_k, k2_sem), (1, put_v, v2_sem)):
        pltpu.make_async_copy(put.at[pl.ds(4 * g, 4)], cache_ref.at[0, :, c, mine, :], own_sem.at[c]).wait()
        wait_bytes(put.at[pl.ds(0, 4 * (groups - 1))], sent_sem.at[2 + c])
        wait_bytes(put.at[pl.ds(0, 4 * (groups - 1))], sem)


def write_kernel(handed, moved, handed_hbm, moved_hbm, sem):
    copies = [pltpu.make_async_copy(moved.at[0, i], moved_hbm.at[0, i], sem.at[i]) for i in range(4)]
    copies.append(pltpu.make_async_copy(handed, handed_hbm, sem.at[4]))
    for copy in copies:
        copy.start()
    for copy in copies:
        copy.wait()


def shards(nx, nz, nt, queries, kv_cache, new_kv, residual, out_weight, dest_cell, lengths):
    groups = nx * nz
    rows = 2 * groups
    cells = 4 * groups
    ctx = kv_cache.shape[3]
    span = ctx // groups
    width = residual.shape[-1]
    bf = jnp.bfloat16
    f32 = jnp.float32
    dma = pltpu.SemaphoreType.DMA
    vmem = pl.BlockSpec(memory_space=pltpu.VMEM)
    hbm = pl.BlockSpec(memory_space=pltpu.HBM)
    handed, moved = pl.pallas_call(
        functools.partial(move_kernel, nx, nz, nt),
        out_shape=(pltpu.VMEM((1, 4, width), bf), pltpu.VMEM((1, 4, 2, ctx, HD), bf)),
        in_specs=[hbm] * 7,
        out_specs=(vmem, vmem),
        scratch_shapes=[
            pltpu.SMEM((rows,), jnp.int32),
            pltpu.SMEM((rows,), jnp.int32),
            pltpu.VMEM(queries.shape, bf),
            pltpu.VMEM(new_kv.shape, bf),
            pltpu.VMEM(residual.shape, bf),
            pltpu.VMEM((8, cells), jnp.int32),
            pltpu.SMEM((8, cells), jnp.int32),
            pltpu.VMEM((2, 2, ctx, HD), bf),
            pltpu.VMEM(out_weight.shape[1:], bf),
            pltpu.VMEM((rows + 1, span, HD), bf),
            pltpu.VMEM((rows + 1, span, HD), bf),
            pltpu.VMEM((cells, span, HD), bf),
            pltpu.VMEM((cells, span, HD), bf),
            pltpu.VMEM((nt, 2, width), f32),
            pltpu.VMEM((nt, 2, width), f32),
            pltpu.VMEM((2, 1, width), f32),
            pltpu.VMEM((rows, 1, width), f32),
            dma, dma((5,)), dma, dma, dma((2,)), dma((4,)), dma, dma, dma, dma, dma, dma, dma, dma, dma, dma,
        ],
        compiler_params=pltpu.CompilerParams(
            collective_id=0, has_side_effects=True, vmem_limit_bytes=60 * 1024 * 1024
        ),
    )(dest_cell, lengths, queries, kv_cache, new_kv, residual, out_weight)
    return pl.pallas_call(
        write_kernel,
        out_shape=(
            jax.ShapeDtypeStruct(handed.shape, bf),
            jax.ShapeDtypeStruct(moved.shape, bf),
        ),
        in_specs=[vmem, vmem],
        out_specs=(hbm, hbm),
        scratch_shapes=[dma((5,))],
        compiler_params=pltpu.CompilerParams(vmem_limit_bytes=8 * 1024 * 1024),
    )(handed, moved)


def solution(mesh):
    in_specs = (
        P("section", "group", "tensor"),
        P("section", "group", None, None, "tensor"),
        P("section", "group", None, "tensor"),
        P("section", "group", "tensor"),
        P("section", "tensor", None),
        P(),
        P(),
    )
    out_specs = (P("section", "group", "tensor"), P("section", "group", None, None, "tensor"))
    nz = min(NZ, mesh.shape["group"] // 2)
    body = functools.partial(shards, mesh.shape["group"] // nz, nz, mesh.shape["tensor"])
    return jax.shard_map(body, mesh=mesh, in_specs=in_specs, out_specs=out_specs, check_vma=False)
```

```python
import functools

import jax
import jax.numpy as jnp
from jax import lax
from jax.experimental import pallas as pl
from jax.experimental.pallas import tpu as pltpu
from jax.sharding import PartitionSpec as P

HD = 128
NZ = 8
MESH = pl.DeviceIdType.MESH


def move_kernel(
    nx, nz, nt,
    dest_hbm, len_hbm, q_hbm, kv_hbm, fresh_hbm, res_hbm, w_hbm,
    handed_ref, cache_ref,
    dest_ref, len_ref, q_ref, fresh_ref, res_ref, row_of, row_of_ref,
    kv, w, got_k, got_v, put_k, put_v, part, red, lay_own, lay,
    in_sem, small_sem, row_sem, w_sem, own_sem, sent_sem, k1_sem, v1_sem, k2_sem, v2_sem, red_sent, red_sem, layz_sent, layx_sent, layz_sem, layx_sem,
):
    groups = nx * nz
    ctx = kv.shape[2]
    span = ctx // groups
    rows = 2 * groups
    g = lax.axis_index("group")
    s = lax.axis_index("section")
    t = lax.axis_index("tensor")
    x = g // nz
    z = g % nz

    load_kv = [pltpu.make_async_copy(kv_hbm.at[0, :, c], kv.at[:, c], in_sem.at[c]) for c in range(2)]
    for load in load_kv:
        load.start()
    small = [
        pltpu.make_async_copy(src, dst, small_sem.at[i])
        for i, (src, dst) in enumerate(
            ((len_hbm, len_ref), (fresh_hbm, fresh_ref), (q_hbm, q_ref), (dest_hbm, dest_ref), (res_hbm, res_ref))
        )
    ]
    for load in small:
        load.start()

    barrier = pltpu.get_barrier_semaphore()

    def greet_group(k, carry):
        pl.semaphore_signal(barrier, inc=1, device_id={"group": (g + k) % groups}, device_id_type=MESH)
        return carry

    def greet_tensor(k, carry):
        pl.semaphore_signal(barrier, inc=1, device_id={"tensor": (t + k) % nt}, device_id_type=MESH)
        return carry

    def greet_section(k, carry):
        pl.semaphore_signal(
            barrier, inc=1, device_id={"group": x * nz + (z + k) % nz, "section": 1 - s}, device_id_type=MESH
        )
        return carry

    lax.fori_loop(1, groups, greet_group, 0)
    lax.fori_loop(1, nt, greet_tensor, 0)
    lax.fori_loop(0, nz, greet_section, 0)

    for load in small:
        load.wait()
    len0 = len_ref[2 * g]
    len1 = len_ref[2 * g + 1]
    pos = lax.broadcasted_iota(jnp.int32, (ctx, HD), 0)
    mine = pl.ds(pl.multiple_of(span * g, span), span)

    def append(c, got):
        load_kv[c].wait()
        for r, n in ((0, len0), (1, len1)):
            token = jnp.broadcast_to(fresh_ref[0, r, c : c + 1, :].astype(jnp.float32), (ctx, HD))
            kv[r, c] = jnp.where(pos == n, token, kv[r, c].astype(jnp.float32)).astype(jnp.bfloat16)
            got[2 * g + r] = kv[r, c, mine, :]
        got[rows] = jnp.zeros((span, HD), jnp.bfloat16)

    cells = row_of.shape[1]
    cell = lax.broadcasted_iota(jnp.int32, (8, cells), 1)

    def place(r, found):
        return jnp.where(cell == dest_ref[r], r, found)

    found = lax.fori_loop(0, rows, place, jnp.full((8, cells), rows, jnp.int32), unroll=8)
    row_of[...] = found
    load_row_of = pltpu.make_async_copy(row_of, row_of_ref, row_sem)
    load_row_of.start()

    append(0, got_k)
    load_w = pltpu.make_async_copy(w_hbm.at[0], w, w_sem)
    load_w.start()
    pl.semaphore_wait(barrier, groups - 1 + nt - 1 + nz)

    z_offsets = [o for m in range(nz // 2 - 1, 0, -1) for o in (m, nz - m)]
    z_offsets[2:2] = [nz // 2]
    z_offsets.append(0)

    def for_partners(low, high, send):
        def window(v, carry):
            for j, dz in enumerate(z_offsets):
                dx = (j + v) % nx
                d = ((x + dx) % nx) * nz + (z + dz) % nz
                if dz == 0:
                    pl.when(dx != 0)(functools.partial(send, d))
                else:
                    send(d)
            return carry

        lax.fori_loop(low, high, window, 0)

    def hop1(c, dst, sem, low, high):
        def send(d):
            pltpu.make_async_remote_copy(
                src_ref=kv.at[:, c, pl.ds(pl.multiple_of(span * d, span), span), :],
                dst_ref=dst.at[pl.ds(2 * g, 2)],
                send_sem=sent_sem.at[c],
                recv_sem=sem,
                device_id={"group": d},
                device_id_type=MESH,
            ).start()

        for_partners(low, high, send)

    hop1(0, got_k, k1_sem, 0, nx)
    append(1, got_v)

    qf = q_ref[0].astype(jnp.float32)
    q8 = jnp.concatenate(
        [qf[r : r + 1, h * HD : (h + 1) * HD] for r in range(2) for h in range(4)], axis=0
    ).astype(jnp.bfloat16)
    dims = (((1,), (1,)), ((), ()))
    first = lax.broadcasted_iota(jnp.int32, (8, ctx), 0) < 4
    scores = jnp.where(
        first,
        lax.dot_general(q8, kv[0, 0], dims, preferred_element_type=jnp.float32),
        lax.dot_general(q8, kv[1, 0], dims, preferred_element_type=jnp.float32),
    ) * (1.0 / HD**0.5)
    valid = lax.broadcasted_iota(jnp.int32, (8, ctx), 1) <= jnp.where(first, len0, len1)
    scores = jnp.where(valid, scores, -1e30)
    top = jnp.max(scores, axis=1, keepdims=True)
    e = jnp.where(valid, jnp.exp(scores - top), 0.0)
    weights = (e / jnp.sum(e, axis=1, keepdims=True)).astype(jnp.bfloat16)
    sub = lax.broadcasted_iota(jnp.int32, (8, HD), 0)
    attended = jnp.where(
        sub < 4,
        jnp.dot(weights, kv[0, 1], preferred_element_type=jnp.float32),
        jnp.dot(weights, kv[1, 1], preferred_element_type=jnp.float32),
    )
    lhs = jnp.concatenate(
        [jnp.where(sub % 4 == h, attended, 0.0) for h in range(4)], axis=1
    ).astype(jnp.bfloat16)

    def wait_bytes(ref, sem):
        pltpu.make_async_copy(ref, ref, sem).wait()

    def hop2(c, got, put, sem, low, high):
        def copy_slots(d):
            for slot in range(4):
                put[4 * d + slot] = got[row_of_ref[0, 4 * d + slot]]

        def send(d):
            copy_slots(d)
            pltpu.make_async_remote_copy(
                src_ref=put.at[pl.ds(4 * d, 4)],
                dst_ref=cache_ref.at[0, :, c, mine, :],
                send_sem=sent_sem.at[2 + c],
                recv_sem=sem,
                device_id={"group": d},
                device_id_type=MESH,
            ).start()

        for_partners(low, high, send)
        if high == nx:
            copy_slots(g)
            pltpu.make_async_copy(put.at[pl.ds(4 * g, 4)], cache_ref.at[0, :, c, mine, :], own_sem.at[c]).start()

    hop1(1, got_v, v1_sem, 0, nx // 2)

    width = res_ref.shape[2]
    load_w.wait()

    def project(k, carry):
        d = (t + k) % nt
        cols = pl.ds(pl.multiple_of(width * d, width), width)
        p8 = jnp.dot(lhs, w[:, cols], preferred_element_type=jnp.float32)
        both = jnp.concatenate(
            [jnp.sum(p8[0:4], axis=0, keepdims=True), jnp.sum(p8[4:8], axis=0, keepdims=True)], axis=0
        )
        part[d] = both

        @pl.when(k < nt)
        def _():
            pltpu.make_async_remote_copy(
                src_ref=part.at[d],
                dst_ref=red.at[t],
                send_sem=red_sent,
                recv_sem=red_sem,
                device_id={"tensor": d},
                device_id_type=MESH,
            ).start()

        return carry

    lax.fori_loop(1, nt + 1, project, 0)
    red[t] = part[t]

    hop1(1, got_v, v1_sem, nx // 2, nx)

    load_row_of.wait()
    wait_bytes(got_k.at[pl.ds(0, rows - 2)], k1_sem)
    hop2(0, got_k, put_k, k2_sem, 0, nx // 2)

    wait_bytes(red.at[pl.ds(0, nt - 1)], red_sem)
    total = red[0]
    for i in range(1, nt):
        total = total + red[i]
    total = total + res_ref[0].astype(jnp.float32)
    lay_own[0] = total[0:1]
    lay_own[1] = total[1:2]

    def hand(k, carry):
        pltpu.make_async_remote_copy(
            src_ref=lay_own,
            dst_ref=lay.at[pl.ds(2 * g, 2)],
            send_sem=layz_sent,
            recv_sem=layz_sem,
            device_id={"group": x * nz + (z + k) % nz, "section": 1 - s},
            device_id_type=MESH,
        ).start()
        return carry

    lax.fori_loop(0, nz, hand, 0)

    hop2(0, got_k, put_k, k2_sem, nx // 2, nx)

    ring = pl.ds(2 * nz * x, 2 * nz)
    wait_bytes(lay.at[pl.ds(0, 2 * nz)], layz_sem)

    def spread(k, carry):
        pltpu.make_async_remote_copy(
            src_ref=lay.at[ring],
            dst_ref=lay.at[ring],
            send_sem=layx_sent,
            recv_sem=layx_sem,
            device_id={"group": ((x + k) % nx) * nz + z},
            device_id_type=MESH,
        ).start()
        return carry

    lax.fori_loop(1, nx, spread, 0)

    wait_bytes(got_v.at[pl.ds(0, rows - 2)], v1_sem)
    hop2(1, got_v, put_v, v2_sem, 0, nx)

    wait_bytes(lay.at[pl.ds(0, 2 * nz * (nx - 1))], layx_sem)
    out_rows = []
    for slot in range(4):
        r = row_of_ref[0, 4 * g + slot]
        out_rows.append(jnp.where(r < rows, lay[jnp.minimum(r, rows - 1)], 0.0))
    handed_ref[0] = jnp.concatenate(out_rows, axis=0).astype(jnp.bfloat16)

    wait_bytes(part.at[pl.ds(0, nt - 1)], red_sent)
    wait_bytes(lay.at[pl.ds(0, 2 * nz)], layz_sent)
    wait_bytes(lay.at[pl.ds(0, 2 * nz * (nx - 1))], layx_sent)
    wait_bytes(got_k.at[pl.ds(0, rows - 2)], sent_sem.at[0])
    wait_bytes(got_v.at[pl.ds(0, rows - 2)], sent_sem.at[1])
    for c, put, sem in ((0, put_k, k2_sem), (1, put_v, v2_sem)):
        pltpu.make_async_copy(put.at[pl.ds(4 * g, 4)], cache_ref.at[0, :, c, mine, :], own_sem.at[c]).wait()
        wait_bytes(put.at[pl.ds(0, 4 * (groups - 1))], sent_sem.at[2 + c])
        wait_bytes(put.at[pl.ds(0, 4 * (groups - 1))], sem)


def write_kernel(handed, moved, handed_hbm, moved_hbm, sem):
    copies = [pltpu.make_async_copy(moved.at[0, i], moved_hbm.at[0, i], sem.at[i]) for i in range(4)]
    copies.append(pltpu.make_async_copy(handed, handed_hbm, sem.at[4]))
    for copy in copies:
        copy.start()
    for copy in copies:
        copy.wait()


def shards(nx, nz, nt, queries, kv_cache, new_kv, residual, out_weight, dest_cell, lengths):
    groups = nx * nz
    rows = 2 * groups
    cells = 4 * groups
    ctx = kv_cache.shape[3]
    span = ctx // groups
    width = residual.shape[-1]
    bf = jnp.bfloat16
    f32 = jnp.float32
    dma = pltpu.SemaphoreType.DMA
    vmem = pl.BlockSpec(memory_space=pltpu.VMEM)
    hbm = pl.BlockSpec(memory_space=pltpu.HBM)
    handed, moved = pl.pallas_call(
        functools.partial(move_kernel, nx, nz, nt),
        out_shape=(pltpu.VMEM((1, 4, width), bf), pltpu.VMEM((1, 4, 2, ctx, HD), bf)),
        in_specs=[hbm] * 7,
        out_specs=(vmem, vmem),
        scratch_shapes=[
            pltpu.SMEM((rows,), jnp.int32),
            pltpu.SMEM((rows,), jnp.int32),
            pltpu.VMEM(queries.shape, bf),
            pltpu.VMEM(new_kv.shape, bf),
            pltpu.VMEM(residual.shape, bf),
            pltpu.VMEM((8, cells), jnp.int32),
            pltpu.SMEM((8, cells), jnp.int32),
            pltpu.VMEM((2, 2, ctx, HD), bf),
            pltpu.VMEM(out_weight.shape[1:], bf),
            pltpu.VMEM((rows + 1, span, HD), bf),
            pltpu.VMEM((rows + 1, span, HD), bf),
            pltpu.VMEM((cells, span, HD), bf),
            pltpu.VMEM((cells, span, HD), bf),
            pltpu.VMEM((nt, 2, width), f32),
            pltpu.VMEM((nt, 2, width), f32),
            pltpu.VMEM((2, 1, width), f32),
            pltpu.VMEM((rows, 1, width), f32),
            dma((2,)), dma((5,)), dma, dma, dma((2,)), dma((4,)), dma, dma, dma, dma, dma, dma, dma, dma, dma, dma,
        ],
        compiler_params=pltpu.CompilerParams(
            collective_id=0, has_side_effects=True, vmem_limit_bytes=60 * 1024 * 1024
        ),
    )(dest_cell, lengths, queries, kv_cache, new_kv, residual, out_weight)
    return pl.pallas_call(
        write_kernel,
        out_shape=(
            jax.ShapeDtypeStruct(handed.shape, bf),
            jax.ShapeDtypeStruct(moved.shape, bf),
        ),
        in_specs=[vmem, vmem],
        out_specs=(hbm, hbm),
        scratch_shapes=[dma((5,))],
        compiler_params=pltpu.CompilerParams(vmem_limit_bytes=8 * 1024 * 1024),
    )(handed, moved)


def solution(mesh):
    in_specs = (
        P("section", "group", "tensor"),
        P("section", "group", None, None, "tensor"),
        P("section", "group", None, "tensor"),
        P("section", "group", "tensor"),
        P("section", "tensor", None),
        P(),
        P(),
    )
    out_specs = (P("section", "group", "tensor"), P("section", "group", None, None, "tensor"))
    nz = min(NZ, mesh.shape["group"] // 2)
    body = functools.partial(shards, mesh.shape["group"] // nz, nz, mesh.shape["tensor"])
    return jax.shard_map(body, mesh=mesh, in_specs=in_specs, out_specs=out_specs, check_vma=False)
```

```python
import functools

import jax
import jax.numpy as jnp
from jax import lax
from jax.experimental import pallas as pl
from jax.experimental.pallas import tpu as pltpu
from jax.sharding import PartitionSpec as P

HD = 128
NZ = 8
MESH = pl.DeviceIdType.MESH


def move_kernel(
    nx, nz, nt,
    dest_hbm, len_hbm, q_hbm, kv_hbm, fresh_hbm, res_hbm, w_hbm,
    handed_ref, cache_ref,
    dest_ref, len_ref, q_ref, fresh_ref, res_ref, row_of, row_of_ref,
    kv, w, got_k, got_v, put_k, put_v, part, red, lay_own, lay,
    in_sem, small_sem, row_sem, w_sem, own_sem, sent_sem, k1_sem, v1_sem, k2_sem, v2_sem, red_sent, red_sem, layz_sent, layx_sent, layz_sem, layx_sem,
):
    groups = nx * nz
    span = kv.shape[3]
    ctx = span * groups
    rows = 2 * groups
    g = lax.axis_index("group")
    s = lax.axis_index("section")
    t = lax.axis_index("tensor")
    x = g // nz
    z = g % nz

    load_kv = [
        [pltpu.make_async_copy(kv_hbm.at[0, r, c], kv.at[c, :, r], in_sem.at[c, r]) for r in range(2)]
        for c in range(2)
    ]
    for c in range(2):
        for load in load_kv[c]:
            load.start()
    small = [
        pltpu.make_async_copy(src, dst, small_sem.at[i])
        for i, (src, dst) in enumerate(
            ((len_hbm, len_ref), (fresh_hbm, fresh_ref), (q_hbm, q_ref), (dest_hbm, dest_ref), (res_hbm, res_ref))
        )
    ]
    for load in small:
        load.start()

    barrier = pltpu.get_barrier_semaphore()

    def greet_group(k, carry):
        pl.semaphore_signal(barrier, inc=1, device_id={"group": (g + k) % groups}, device_id_type=MESH)
        return carry

    def greet_tensor(k, carry):
        pl.semaphore_signal(barrier, inc=1, device_id={"tensor": (t + k) % nt}, device_id_type=MESH)
        return carry

    def greet_section(k, carry):
        pl.semaphore_signal(
            barrier, inc=1, device_id={"group": x * nz + (z + k) % nz, "section": 1 - s}, device_id_type=MESH
        )
        return carry

    lax.fori_loop(1, groups, greet_group, 0)
    lax.fori_loop(1, nt, greet_tensor, 0)
    lax.fori_loop(0, nz, greet_section, 0)

    load_len, load_fresh, *load_rest = small
    load_len.wait()
    load_fresh.wait()
    len0 = len_ref[2 * g]
    len1 = len_ref[2 * g + 1]
    chunks = (groups, span, HD)
    pos = lax.broadcasted_iota(jnp.int32, chunks, 0) * span + lax.broadcasted_iota(jnp.int32, chunks, 1)

    def append(c, got):
        for r, n in ((0, len0), (1, len1)):
            load_kv[c][r].wait()
            token = jnp.broadcast_to(fresh_ref[0, r, c : c + 1, :].astype(jnp.float32)[None], chunks)
            kv[c, :, r] = jnp.where(pos == n, token, kv[c, :, r].astype(jnp.float32)).astype(jnp.bfloat16)
            got[2 * g + r] = kv[c, g, r]
        got[rows] = jnp.zeros((span, HD), jnp.bfloat16)

    append(0, got_k)
    load_w = pltpu.make_async_copy(w_hbm.at[0], w, w_sem)
    load_w.start()
    pl.semaphore_wait(barrier, groups - 1 + nt - 1 + nz)

    z_offsets = [o for m in range(nz // 2 - 1, 0, -1) for o in (m, nz - m)]
    z_offsets[2:2] = [nz // 2]
    z_offsets.append(0)

    way = 1 - 2 * s

    def for_partners(low, high, send):
        def window(v, carry):
            for j, dz in enumerate(z_offsets):
                dx = (j + v) % nx
                d = ((x + way * dx + nx) % nx) * nz + (z + way * dz + nz) % nz
                if dz == 0:
                    pl.when(dx != 0)(functools.partial(send, d))
                else:
                    send(d)
            return carry

        lax.fori_loop(low, high, window, 0)

    def hop1(c, dst, sem, low, high):
        def send(d):
            pltpu.make_async_remote_copy(
                src_ref=kv.at[c, d],
                dst_ref=dst.at[pl.ds(2 * g, 2)],
                send_sem=sent_sem.at[c],
                recv_sem=sem,
                device_id={"group": d},
                device_id_type=MESH,
            ).start()

        for_partners(low, high, send)

    hop1(0, got_k, k1_sem, 0, nx)
    append(1, got_v)

    for load in load_rest:
        load.wait()
    cells = row_of.shape[1]
    cell = lax.broadcasted_iota(jnp.int32, (8, cells), 1)

    def place(r, found):
        return jnp.where(cell == dest_ref[r], r, found)

    found = lax.fori_loop(0, rows, place, jnp.full((8, cells), rows, jnp.int32), unroll=8)
    row_of[...] = found
    load_row_of = pltpu.make_async_copy(row_of, row_of_ref, row_sem)
    load_row_of.start()

    qf = q_ref[0].astype(jnp.float32)
    q8 = jnp.concatenate(
        [qf[r : r + 1, h * HD : (h + 1) * HD] for r in range(2) for h in range(4)], axis=0
    ).astype(jnp.bfloat16)
    dims = (((1,), (1,)), ((), ()))

    def cached(c, r):
        return kv[c, :, r].reshape(ctx, HD)

    first = lax.broadcasted_iota(jnp.int32, (8, ctx), 0) < 4
    scores = jnp.where(
        first,
        lax.dot_general(q8, cached(0, 0), dims, preferred_element_type=jnp.float32),
        lax.dot_general(q8, cached(0, 1), dims, preferred_element_type=jnp.float32),
    ) * (1.0 / HD**0.5)
    valid = lax.broadcasted_iota(jnp.int32, (8, ctx), 1) <= jnp.where(first, len0, len1)
    scores = jnp.where(valid, scores, -1e30)
    top = jnp.max(scores, axis=1, keepdims=True)
    e = jnp.where(valid, jnp.exp(scores - top), 0.0)
    weights = (e / jnp.sum(e, axis=1, keepdims=True)).astype(jnp.bfloat16)
    sub = lax.broadcasted_iota(jnp.int32, (8, HD), 0)
    attended = jnp.where(
        sub < 4,
        jnp.dot(weights, cached(1, 0), preferred_element_type=jnp.float32),
        jnp.dot(weights, cached(1, 1), preferred_element_type=jnp.float32),
    )
    lhs = jnp.concatenate(
        [jnp.where(sub % 4 == h, attended, 0.0) for h in range(4)], axis=1
    ).astype(jnp.bfloat16)

    def wait_bytes(ref, sem):
        pltpu.make_async_copy(ref, ref, sem).wait()

    def hop2(c, got, put, sem, low, high):
        def copy_slots(d):
            for slot in range(4):
                put[4 * d + slot] = got[row_of_ref[0, 4 * d + slot]]

        def send(d):
            copy_slots(d)
            pltpu.make_async_remote_copy(
                src_ref=put.at[pl.ds(4 * d, 4)],
                dst_ref=cache_ref.at[c, g],
                send_sem=sent_sem.at[2 + c],
                recv_sem=sem,
                device_id={"group": d},
                device_id_type=MESH,
            ).start()

        for_partners(low, high, send)
        if high == nx:
            copy_slots(g)
            pltpu.make_async_copy(put.at[pl.ds(4 * g, 4)], cache_ref.at[c, g], own_sem.at[c]).start()

    hop1(1, got_v, v1_sem, 0, nx // 2)

    width = res_ref.shape[2]
    load_w.wait()

    def project(k, carry):
        d = (t + k) % nt
        cols = pl.ds(pl.multiple_of(width * d, width), width)
        p8 = jnp.dot(lhs, w[:, cols], preferred_element_type=jnp.float32)
        both = jnp.concatenate(
            [jnp.sum(p8[0:4], axis=0, keepdims=True), jnp.sum(p8[4:8], axis=0, keepdims=True)], axis=0
        )
        part[d] = both

        @pl.when(k < nt)
        def _():
            pltpu.make_async_remote_copy(
                src_ref=part.at[d],
                dst_ref=red.at[t],
                send_sem=red_sent,
                recv_sem=red_sem,
                device_id={"tensor": d},
                device_id_type=MESH,
            ).start()

        return carry

    lax.fori_loop(1, nt + 1, project, 0)
    red[t] = part[t]

    hop1(1, got_v, v1_sem, nx // 2, nx)

    load_row_of.wait()
    wait_bytes(got_k.at[pl.ds(0, rows - 2)], k1_sem)
    hop2(0, got_k, put_k, k2_sem, 0, nx // 2)

    wait_bytes(red.at[pl.ds(0, nt - 1)], red_sem)
    total = red[0]
    for i in range(1, nt):
        total = total + red[i]
    total = total + res_ref[0].astype(jnp.float32)
    lay_own[...] = total.astype(jnp.bfloat16)

    def hand(k, carry):
        pltpu.make_async_remote_copy(
            src_ref=lay_own,
            dst_ref=lay.at[g],
            send_sem=layz_sent,
            recv_sem=layz_sem,
            device_id={"group": x * nz + (z + k) % nz, "section": 1 - s},
            device_id_type=MESH,
        ).start()
        return carry

    lax.fori_loop(0, nz, hand, 0)

    hop2(0, got_k, put_k, k2_sem, nx // 2, nx)

    ring = pl.ds(nz * x, nz)
    wait_bytes(lay.at[pl.ds(0, nz)], layz_sem)

    def spread(k, carry):
        pltpu.make_async_remote_copy(
            src_ref=lay.at[ring],
            dst_ref=lay.at[ring],
            send_sem=layx_sent,
            recv_sem=layx_sem,
            device_id={"group": ((x + k) % nx) * nz + z},
            device_id_type=MESH,
        ).start()
        return carry

    lax.fori_loop(1, nx, spread, 0)

    wait_bytes(got_v.at[pl.ds(0, rows - 2)], v1_sem)
    hop2(1, got_v, put_v, v2_sem, 0, nx)

    wait_bytes(lay.at[pl.ds(0, nz * (nx - 1))], layx_sem)
    out_rows = []
    for slot in range(4):
        r = row_of_ref[0, 4 * g + slot]
        both = lay[jnp.minimum(r, rows - 1) // 2].astype(jnp.float32)
        out_rows.append(jnp.where(r < rows, jnp.where(r % 2 == 0, both[0:1], both[1:2]), 0.0))
    handed_ref[0] = jnp.concatenate(out_rows, axis=0).astype(jnp.bfloat16)

    wait_bytes(part.at[pl.ds(0, nt - 1)], red_sent)
    wait_bytes(lay.at[pl.ds(0, nz)], layz_sent)
    wait_bytes(lay.at[pl.ds(0, nz * (nx - 1))], layx_sent)
    wait_bytes(got_k.at[pl.ds(0, rows - 2)], sent_sem.at[0])
    wait_bytes(got_v.at[pl.ds(0, rows - 2)], sent_sem.at[1])
    for c, put, sem in ((0, put_k, k2_sem), (1, put_v, v2_sem)):
        pltpu.make_async_copy(put.at[pl.ds(4 * g, 4)], cache_ref.at[c, g], own_sem.at[c]).wait()
        wait_bytes(put.at[pl.ds(0, 4 * (groups - 1))], sent_sem.at[2 + c])
        wait_bytes(put.at[pl.ds(0, 4 * (groups - 1))], sem)


def write_kernel(handed, moved, handed_hbm, moved_hbm, sem):
    copies = [
        pltpu.make_async_copy(moved.at[c, :, i], moved_hbm.at[0, i, c], sem.at[2 * i + c])
        for i in range(4)
        for c in range(2)
    ]
    copies.append(pltpu.make_async_copy(handed, handed_hbm, sem.at[8]))
    for copy in copies:
        copy.start()
    for copy in copies:
        copy.wait()


def shards(nx, nz, nt, queries, kv_cache, new_kv, residual, out_weight, dest_cell, lengths):
    groups = nx * nz
    rows = 2 * groups
    cells = 4 * groups
    ctx = kv_cache.shape[3]
    span = ctx // groups
    width = residual.shape[-1]
    bf = jnp.bfloat16
    f32 = jnp.float32
    dma = pltpu.SemaphoreType.DMA
    vmem = pl.BlockSpec(memory_space=pltpu.VMEM)
    hbm = pl.BlockSpec(memory_space=pltpu.HBM)
    handed, moved = pl.pallas_call(
        functools.partial(move_kernel, nx, nz, nt),
        out_shape=(pltpu.VMEM((1, 4, width), bf), pltpu.VMEM((2, groups, 4, span, HD), bf)),
        in_specs=[hbm] * 7,
        out_specs=(vmem, vmem),
        scratch_shapes=[
            pltpu.SMEM((rows,), jnp.int32),
            pltpu.SMEM((rows,), jnp.int32),
            pltpu.VMEM(queries.shape, bf),
            pltpu.VMEM(new_kv.shape, bf),
            pltpu.VMEM(residual.shape, bf),
            pltpu.VMEM((8, cells), jnp.int32),
            pltpu.SMEM((8, cells), jnp.int32),
            pltpu.VMEM((2, groups, 2, span, HD), bf),
            pltpu.VMEM(out_weight.shape[1:], bf),
            pltpu.VMEM((rows + 1, span, HD), bf),
            pltpu.VMEM((rows + 1, span, HD), bf),
            pltpu.VMEM((cells, span, HD), bf),
            pltpu.VMEM((cells, span, HD), bf),
            pltpu.VMEM((nt, 2, width), f32),
            pltpu.VMEM((nt, 2, width), f32),
            pltpu.VMEM((2, width), bf),
            pltpu.VMEM((groups, 2, width), bf),
            dma((2, 2)), dma((5,)), dma, dma, dma((2,)), dma((4,)), dma, dma, dma, dma, dma, dma, dma, dma, dma, dma,
        ],
        compiler_params=pltpu.CompilerParams(
            collective_id=0, has_side_effects=True, vmem_limit_bytes=60 * 1024 * 1024
        ),
    )(dest_cell, lengths, queries, kv_cache.reshape(1, 2, 2, groups, span, HD), new_kv, residual, out_weight)
    handed, moved = pl.pallas_call(
        write_kernel,
        out_shape=(
            jax.ShapeDtypeStruct(handed.shape, bf),
            jax.ShapeDtypeStruct((1, 4, 2, groups, span, HD), bf),
        ),
        in_specs=[vmem, vmem],
        out_specs=(hbm, hbm),
        scratch_shapes=[dma((9,))],
        compiler_params=pltpu.CompilerParams(vmem_limit_bytes=8 * 1024 * 1024),
    )(handed, moved)
    return handed, moved.reshape(1, 4, 2, ctx, HD)


def solution(mesh):
    in_specs = (
        P("section", "group", "tensor"),
        P("section", "group", None, None, "tensor"),
        P("section", "group", None, "tensor"),
        P("section", "group", "tensor"),
        P("section", "tensor", None),
        P(),
        P(),
    )
    out_specs = (P("section", "group", "tensor"), P("section", "group", None, None, "tensor"))
    nz = min(NZ, mesh.shape["group"] // 2)
    body = functools.partial(shards, mesh.shape["group"] // nz, nz, mesh.shape["tensor"])
    return jax.shard_map(body, mesh=mesh, in_specs=in_specs, out_specs=out_specs, check_vma=False)
```

```python
import functools

import jax
import jax.numpy as jnp
from jax import lax
from jax.experimental import pallas as pl
from jax.experimental.pallas import tpu as pltpu
from jax.sharding import PartitionSpec as P

HD = 128
NZ = 8
MESH = pl.DeviceIdType.MESH


def move_kernel(
    nx, nz, nt,
    dest_hbm, len_hbm, q_hbm, kv_hbm, fresh_hbm, res_hbm, w_hbm,
    handed_ref, cache_ref,
    dest_ref, len_ref, q_ref, fresh_ref, res_ref, row_of, row_of_ref,
    kv, w, got_k, got_v, put_k, put_v, part, red, lay_own, lay,
    in_sem, small_sem, row_sem, w_sem, own_sem, sent_sem, k1_sem, v1_sem, k2_sem, v2_sem, red_sent, red_sem, layz_sent, layx_sent, layz_sem, layx_sem,
):
    groups = nx * nz
    ctx = kv.shape[2]
    span = ctx // groups
    rows = 2 * groups
    g = lax.axis_index("group")
    s = lax.axis_index("section")
    t = lax.axis_index("tensor")
    x = lax.div(g, nz)
    z = lax.rem(g, nz)

    load_kv = [pltpu.make_async_copy(kv_hbm.at[0, :, c], kv.at[:, c], in_sem.at[c]) for c in range(2)]
    for load in load_kv:
        load.start()
    small = [
        pltpu.make_async_copy(src, dst, small_sem.at[i])
        for i, (src, dst) in enumerate(
            ((len_hbm, len_ref), (fresh_hbm, fresh_ref), (q_hbm, q_ref), (dest_hbm, dest_ref), (res_hbm, res_ref))
        )
    ]
    for load in small:
        load.start()

    barrier = pltpu.get_barrier_semaphore()

    def greet_group(k, carry):
        pl.semaphore_signal(barrier, inc=1, device_id={"group": lax.rem(g + k, groups)}, device_id_type=MESH)
        return carry

    def greet_tensor(k, carry):
        pl.semaphore_signal(barrier, inc=1, device_id={"tensor": lax.rem(t + k, nt)}, device_id_type=MESH)
        return carry

    def greet_section(k, carry):
        pl.semaphore_signal(
            barrier, inc=1, device_id={"group": x * nz + lax.rem(z + k, nz), "section": 1 - s}, device_id_type=MESH
        )
        return carry

    lax.fori_loop(1, groups, greet_group, 0)
    lax.fori_loop(1, nt, greet_tensor, 0)
    lax.fori_loop(0, nz, greet_section, 0)

    load_len, load_fresh, *load_rest = small
    load_len.wait()
    load_fresh.wait()
    len0 = len_ref[2 * g]
    len1 = len_ref[2 * g + 1]
    pos = lax.broadcasted_iota(jnp.int32, (ctx, HD), 0)
    mine = pl.ds(pl.multiple_of(span * g, span), span)

    def append(c, got):
        load_kv[c].wait()
        for r, n in ((0, len0), (1, len1)):
            token = jnp.broadcast_to(fresh_ref[0, r, c : c + 1, :].astype(jnp.float32), (ctx, HD))
            kv[r, c] = jnp.where(pos == n, token, kv[r, c].astype(jnp.float32)).astype(jnp.bfloat16)
            got[2 * g + r] = kv[r, c, mine, :]
        got[rows] = jnp.zeros((span, HD), jnp.bfloat16)

    append(0, got_k)
    load_w = pltpu.make_async_copy(w_hbm.at[0], w, w_sem)
    load_w.start()
    pl.semaphore_wait(barrier, groups - 1 + nt - 1 + nz)

    z_offsets = [o for m in range(nz // 2 - 1, 0, -1) for o in (m, nz - m)]
    z_offsets[2:2] = [nz // 2]
    z_offsets.append(0)

    way = 1 - 2 * s

    z_partners = [lax.rem(z + way * dz + nz, nz) for dz in z_offsets]

    def for_partners(low, high, send):
        def window(v, carry):
            for j, dz in enumerate(z_offsets):
                d = lax.rem(x + way * (j + v) + nx * nz, nx) * nz + z_partners[j]
                if dz == 0:
                    pl.when(lax.rem(j + v, nx) != 0)(functools.partial(send, d))
                else:
                    send(d)
            return carry

        lax.fori_loop(low, high, window, 0)

    def hop1(c, dst, sem, low, high):
        def send(d):
            pltpu.make_async_remote_copy(
                src_ref=kv.at[:, c, pl.ds(pl.multiple_of(span * d, span), span), :],
                dst_ref=dst.at[pl.ds(2 * g, 2)],
                send_sem=sent_sem.at[c],
                recv_sem=sem,
                device_id={"group": d},
                device_id_type=MESH,
            ).start()

        for_partners(low, high, send)

    hop1(0, got_k, k1_sem, 0, nx)
    append(1, got_v)
    hop1(1, got_v, v1_sem, 0, nx)

    for load in load_rest:
        load.wait()
    cells = row_of.shape[1]
    cell = lax.broadcasted_iota(jnp.int32, (8, cells), 1)

    def place(r, found):
        return jnp.where(cell == dest_ref[r], r, found)

    found = lax.fori_loop(0, rows, place, jnp.full((8, cells), rows, jnp.int32), unroll=8)
    row_of[...] = found
    load_row_of = pltpu.make_async_copy(row_of, row_of_ref, row_sem)
    load_row_of.start()

    qf = q_ref[0].astype(jnp.float32)
    q8 = jnp.concatenate(
        [qf[r : r + 1, h * HD : (h + 1) * HD] for r in range(2) for h in range(4)], axis=0
    ).astype(jnp.bfloat16)
    dims = (((1,), (1,)), ((), ()))
    first = lax.broadcasted_iota(jnp.int32, (8, ctx), 0) < 4
    scores = jnp.where(
        first,
        lax.dot_general(q8, kv[0, 0], dims, preferred_element_type=jnp.float32),
        lax.dot_general(q8, kv[1, 0], dims, preferred_element_type=jnp.float32),
    ) * (1.0 / HD**0.5)
    valid = lax.broadcasted_iota(jnp.int32, (8, ctx), 1) <= jnp.where(first, len0, len1)
    scores = jnp.where(valid, scores, -1e30)
    top = jnp.max(scores, axis=1, keepdims=True)
    e = jnp.where(valid, jnp.exp(scores - top), 0.0)
    weights = (e / jnp.sum(e, axis=1, keepdims=True)).astype(jnp.bfloat16)
    sub = lax.broadcasted_iota(jnp.int32, (8, HD), 0)
    attended = jnp.where(
        sub < 4,
        jnp.dot(weights, kv[0, 1], preferred_element_type=jnp.float32),
        jnp.dot(weights, kv[1, 1], preferred_element_type=jnp.float32),
    )
    lhs = jnp.concatenate(
        [jnp.where(sub % 4 == h, attended, 0.0) for h in range(4)], axis=1
    ).astype(jnp.bfloat16)

    def wait_bytes(ref, sem):
        pltpu.make_async_copy(ref, ref, sem).wait()

    def hop2(c, got, put, sem, low, high):
        def copy_slots(d):
            for slot in range(4):
                put[4 * d + slot] = got[row_of_ref[0, 4 * d + slot]]

        def send(d):
            copy_slots(d)
            pltpu.make_async_remote_copy(
                src_ref=put.at[pl.ds(4 * d, 4)],
                dst_ref=cache_ref.at[0, :, c, mine, :],
                send_sem=sent_sem.at[2 + c],
                recv_sem=sem,
                device_id={"group": d},
                device_id_type=MESH,
            ).start()

        for_partners(low, high, send)
        if high == nx:
            copy_slots(g)
            pltpu.make_async_copy(put.at[pl.ds(4 * g, 4)], cache_ref.at[0, :, c, mine, :], own_sem.at[c]).start()

    width = res_ref.shape[2]
    load_w.wait()

    def project(k, carry):
        d = lax.rem(t + k, nt)
        cols = pl.ds(pl.multiple_of(width * d, width), width)
        p8 = jnp.dot(lhs, w[:, cols], preferred_element_type=jnp.float32)
        both = jnp.concatenate(
            [jnp.sum(p8[0:4], axis=0, keepdims=True), jnp.sum(p8[4:8], axis=0, keepdims=True)], axis=0
        )
        part[d] = both

        @pl.when(k < nt)
        def _():
            pltpu.make_async_remote_copy(
                src_ref=part.at[d],
                dst_ref=red.at[t],
                send_sem=red_sent,
                recv_sem=red_sem,
                device_id={"tensor": d},
                device_id_type=MESH,
            ).start()

        return carry

    lax.fori_loop(1, nt + 1, project, 0)
    red[t] = part[t]

    load_row_of.wait()
    wait_bytes(got_k.at[pl.ds(0, rows - 2)], k1_sem)
    hop2(0, got_k, put_k, k2_sem, 0, nx // 2)

    wait_bytes(red.at[pl.ds(0, nt - 1)], red_sem)
    total = red[0]
    for i in range(1, nt):
        total = total + red[i]
    total = total + res_ref[0].astype(jnp.float32)
    lay_own[...] = total.astype(jnp.bfloat16)

    def hand(k, carry):
        pltpu.make_async_remote_copy(
            src_ref=lay_own,
            dst_ref=lay.at[g],
            send_sem=layz_sent,
            recv_sem=layz_sem,
            device_id={"group": x * nz + lax.rem(z + k, nz), "section": 1 - s},
            device_id_type=MESH,
        ).start()
        return carry

    lax.fori_loop(0, nz, hand, 0)

    hop2(0, got_k, put_k, k2_sem, nx // 2, nx)

    ring = pl.ds(nz * x, nz)
    wait_bytes(lay.at[pl.ds(0, nz)], layz_sem)

    def spread(k, carry):
        pltpu.make_async_remote_copy(
            src_ref=lay.at[ring],
            dst_ref=lay.at[ring],
            send_sem=layx_sent,
            recv_sem=layx_sem,
            device_id={"group": lax.rem(x + k, nx) * nz + z},
            device_id_type=MESH,
        ).start()
        return carry

    lax.fori_loop(1, nx, spread, 0)

    wait_bytes(got_v.at[pl.ds(0, rows - 2)], v1_sem)
    hop2(1, got_v, put_v, v2_sem, 0, nx)

    wait_bytes(lay.at[pl.ds(0, nz * (nx - 1))], layx_sem)
    out_rows = []
    for slot in range(4):
        r = row_of_ref[0, 4 * g + slot]
        both = lay[jnp.minimum(r, rows - 1) // 2].astype(jnp.float32)
        out_rows.append(jnp.where(r < rows, jnp.where(r % 2 == 0, both[0:1], both[1:2]), 0.0))
    handed_ref[0] = jnp.concatenate(out_rows, axis=0).astype(jnp.bfloat16)

    wait_bytes(part.at[pl.ds(0, nt - 1)], red_sent)
    wait_bytes(lay.at[pl.ds(0, nz)], layz_sent)
    wait_bytes(lay.at[pl.ds(0, nz * (nx - 1))], layx_sent)
    wait_bytes(got_k.at[pl.ds(0, rows - 2)], sent_sem.at[0])
    wait_bytes(got_v.at[pl.ds(0, rows - 2)], sent_sem.at[1])
    for c, put, sem in ((0, put_k, k2_sem), (1, put_v, v2_sem)):
        pltpu.make_async_copy(put.at[pl.ds(4 * g, 4)], cache_ref.at[0, :, c, mine, :], own_sem.at[c]).wait()
        wait_bytes(put.at[pl.ds(0, 4 * (groups - 1))], sent_sem.at[2 + c])
        wait_bytes(put.at[pl.ds(0, 4 * (groups - 1))], sem)


def write_kernel(handed, moved, handed_hbm, moved_hbm, sem):
    copies = [
        pltpu.make_async_copy(moved.at[0, i, c], moved_hbm.at[0, i, c], sem.at[2 * i + c])
        for i in range(4)
        for c in range(2)
    ]
    copies.append(pltpu.make_async_copy(handed, handed_hbm, sem.at[8]))
    for copy in copies:
        copy.start()
    for copy in copies:
        copy.wait()


def shards(nx, nz, nt, queries, kv_cache, new_kv, residual, out_weight, dest_cell, lengths):
    groups = nx * nz
    rows = 2 * groups
    cells = 4 * groups
    ctx = kv_cache.shape[3]
    span = ctx // groups
    width = residual.shape[-1]
    bf = jnp.bfloat16
    f32 = jnp.float32
    dma = pltpu.SemaphoreType.DMA
    vmem = pl.BlockSpec(memory_space=pltpu.VMEM)
    hbm = pl.BlockSpec(memory_space=pltpu.HBM)
    handed, moved = pl.pallas_call(
        functools.partial(move_kernel, nx, nz, nt),
        out_shape=(pltpu.VMEM((1, 4, width), bf), pltpu.VMEM((1, 4, 2, ctx, HD), bf)),
        in_specs=[hbm] * 7,
        out_specs=(vmem, vmem),
        scratch_shapes=[
            pltpu.SMEM((rows,), jnp.int32),
            pltpu.SMEM((rows,), jnp.int32),
            pltpu.VMEM(queries.shape, bf),
            pltpu.VMEM(new_kv.shape, bf),
            pltpu.VMEM(residual.shape, bf),
            pltpu.VMEM((8, cells), jnp.int32),
            pltpu.SMEM((8, cells), jnp.int32),
            pltpu.VMEM((2, 2, ctx, HD), bf),
            pltpu.VMEM(out_weight.shape[1:], bf),
            pltpu.VMEM((rows + 1, span, HD), bf),
            pltpu.VMEM((rows + 1, span, HD), bf),
            pltpu.VMEM((cells, span, HD), bf),
            pltpu.VMEM((cells, span, HD), bf),
            pltpu.VMEM((nt, 2, width), f32),
            pltpu.VMEM((nt, 2, width), f32),
            pltpu.VMEM((2, width), bf),
            pltpu.VMEM((groups, 2, width), bf),
            dma((2,)), dma((5,)), dma, dma, dma((2,)), dma((4,)), dma, dma, dma, dma, dma, dma, dma, dma, dma, dma,
        ],
        compiler_params=pltpu.CompilerParams(
            collective_id=0, has_side_effects=True, vmem_limit_bytes=60 * 1024 * 1024
        ),
    )(dest_cell, lengths, queries, kv_cache, new_kv, residual, out_weight)
    return pl.pallas_call(
        write_kernel,
        out_shape=(
            jax.ShapeDtypeStruct(handed.shape, bf),
            jax.ShapeDtypeStruct(moved.shape, bf),
        ),
        in_specs=[vmem, vmem],
        out_specs=(hbm, hbm),
        scratch_shapes=[dma((9,))],
        compiler_params=pltpu.CompilerParams(vmem_limit_bytes=8 * 1024 * 1024),
    )(handed, moved)


def solution(mesh):
    in_specs = (
        P("section", "group", "tensor"),
        P("section", "group", None, None, "tensor"),
        P("section", "group", None, "tensor"),
        P("section", "group", "tensor"),
        P("section", "tensor", None),
        P(),
        P(),
    )
    out_specs = (P("section", "group", "tensor"), P("section", "group", None, None, "tensor"))
    nz = min(NZ, mesh.shape["group"] // 2)
    body = functools.partial(shards, mesh.shape["group"] // nz, nz, mesh.shape["tensor"])
    return jax.shard_map(body, mesh=mesh, in_specs=in_specs, out_specs=out_specs, check_vma=False)
```

```python
import functools

import jax
import jax.numpy as jnp
from jax import lax
from jax.experimental import pallas as pl
from jax.experimental.pallas import tpu as pltpu
from jax.sharding import PartitionSpec as P

HD = 128
NZ = 8
MESH = pl.DeviceIdType.MESH


def move_kernel(
    nx, nz, nt,
    dest_hbm, len_hbm, q_hbm, kv_hbm, fresh_hbm, res_hbm, w_hbm,
    handed_ref, cache_ref,
    dest_ref, len_ref, q_ref, fresh_ref, res_ref, row_of, row_of_ref,
    kv, w, got, put, part, red, lay_own, lay,
    in_sem, small_sem, row_sem, w_sem, own_sem, sent_sem, hop1_sem, hop2_sem, red_sent, red_sem, layz_sent, layx_sent, layz_sem, layx_sem,
):
    groups = nx * nz
    ctx = kv.shape[2]
    span = ctx // groups
    rows = 2 * groups
    g = lax.axis_index("group")
    s = lax.axis_index("section")
    t = lax.axis_index("tensor")
    x = lax.div(g, nz)
    z = lax.rem(g, nz)

    load_kv = pltpu.make_async_copy(kv_hbm.at[0], kv, in_sem)
    load_kv.start()
    small = [
        pltpu.make_async_copy(src, dst, small_sem.at[i])
        for i, (src, dst) in enumerate(
            ((len_hbm, len_ref), (fresh_hbm, fresh_ref), (q_hbm, q_ref), (dest_hbm, dest_ref), (res_hbm, res_ref))
        )
    ]
    load_len, load_fresh, *load_rest = small
    load_len.start()
    load_fresh.start()

    barrier = pltpu.get_barrier_semaphore()

    def greet_group(k, carry):
        pl.semaphore_signal(barrier, inc=1, device_id={"group": lax.rem(g + k, groups)}, device_id_type=MESH)
        return carry

    def greet_tensor(k, carry):
        pl.semaphore_signal(barrier, inc=1, device_id={"tensor": lax.rem(t + k, nt)}, device_id_type=MESH)
        return carry

    def greet_section(k, carry):
        pl.semaphore_signal(
            barrier, inc=1, device_id={"group": x * nz + lax.rem(z + k, nz), "section": 1 - s}, device_id_type=MESH
        )
        return carry

    lax.fori_loop(1, groups, greet_group, 0)
    lax.fori_loop(1, nt, greet_tensor, 0)
    lax.fori_loop(0, nz, greet_section, 0)

    for load in load_rest:
        load.start()
    load_w = pltpu.make_async_copy(w_hbm.at[0], w, w_sem)
    load_w.start()

    load_len.wait()
    load_fresh.wait()
    len0 = len_ref[2 * g]
    len1 = len_ref[2 * g + 1]
    pos = lax.broadcasted_iota(jnp.int32, (ctx, HD), 0)
    mine = pl.ds(pl.multiple_of(span * g, span), span)

    load_kv.wait()
    for r, n in ((0, len0), (1, len1)):
        for c in range(2):
            token = jnp.broadcast_to(fresh_ref[0, r, c : c + 1, :].astype(jnp.float32), (ctx, HD))
            kv[r, c] = jnp.where(pos == n, token, kv[r, c].astype(jnp.float32)).astype(jnp.bfloat16)
            got[2 * g + r, c] = kv[r, c, mine, :]
    got[rows] = jnp.zeros((2, span, HD), jnp.bfloat16)

    pl.semaphore_wait(barrier, groups - 1 + nt - 1 + nz)

    z_offsets = [o for m in range(nz // 2 - 1, 0, -1) for o in (m, nz - m)]
    z_offsets[2:2] = [nz // 2]
    z_offsets.append(0)

    way = 1 - 2 * s

    z_partners = [lax.rem(z + way * dz + nz, nz) for dz in z_offsets]

    def for_partners(low, high, send):
        def window(v, carry):
            for j, dz in enumerate(z_offsets):
                d = lax.rem(x + way * (j + v) + nx * nz, nx) * nz + z_partners[j]
                if dz == 0:
                    pl.when(lax.rem(j + v, nx) != 0)(functools.partial(send, d))
                else:
                    send(d)
            return carry

        lax.fori_loop(low, high, window, 0)

    def hop1(d):
        pltpu.make_async_remote_copy(
            src_ref=kv.at[:, :, pl.ds(pl.multiple_of(span * d, span), span), :],
            dst_ref=got.at[pl.ds(2 * g, 2)],
            send_sem=sent_sem.at[0],
            recv_sem=hop1_sem,
            device_id={"group": d},
            device_id_type=MESH,
        ).start()

    for_partners(0, nx, hop1)

    for load in load_rest:
        load.wait()
    cells = row_of.shape[1]
    cell = lax.broadcasted_iota(jnp.int32, (8, cells), 1)

    def place(r, found):
        return jnp.where(cell == dest_ref[r], r, found)

    found = lax.fori_loop(0, rows, place, jnp.full((8, cells), rows, jnp.int32), unroll=8)
    row_of[...] = found
    load_row_of = pltpu.make_async_copy(row_of, row_of_ref, row_sem)
    load_row_of.start()

    qf = q_ref[0].astype(jnp.float32)
    q8 = jnp.concatenate(
        [qf[r : r + 1, h * HD : (h + 1) * HD] for r in range(2) for h in range(4)], axis=0
    ).astype(jnp.bfloat16)
    dims = (((1,), (1,)), ((), ()))
    first = lax.broadcasted_iota(jnp.int32, (8, ctx), 0) < 4
    scores = jnp.where(
        first,
        lax.dot_general(q8, kv[0, 0], dims, preferred_element_type=jnp.float32),
        lax.dot_general(q8, kv[1, 0], dims, preferred_element_type=jnp.float32),
    ) * (1.0 / HD**0.5)
    valid = lax.broadcasted_iota(jnp.int32, (8, ctx), 1) <= jnp.where(first, len0, len1)
    scores = jnp.where(valid, scores, -1e30)
    top = jnp.max(scores, axis=1, keepdims=True)
    e = jnp.where(valid, jnp.exp(scores - top), 0.0)
    weights = (e / jnp.sum(e, axis=1, keepdims=True)).astype(jnp.bfloat16)
    sub = lax.broadcasted_iota(jnp.int32, (8, HD), 0)
    attended = jnp.where(
        sub < 4,
        jnp.dot(weights, kv[0, 1], preferred_element_type=jnp.float32),
        jnp.dot(weights, kv[1, 1], preferred_element_type=jnp.float32),
    )
    lhs = jnp.concatenate(
        [jnp.where(sub % 4 == h, attended, 0.0) for h in range(4)], axis=1
    ).astype(jnp.bfloat16)

    def wait_bytes(ref, sem):
        pltpu.make_async_copy(ref, ref, sem).wait()

    def copy_slots(d):
        for slot in range(4):
            put[4 * d + slot] = got[row_of_ref[0, 4 * d + slot]]

    def hop2(d):
        copy_slots(d)
        pltpu.make_async_remote_copy(
            src_ref=put.at[pl.ds(4 * d, 4)],
            dst_ref=cache_ref.at[0, :, :, mine, :],
            send_sem=sent_sem.at[1],
            recv_sem=hop2_sem,
            device_id={"group": d},
            device_id_type=MESH,
        ).start()

    width = res_ref.shape[2]
    load_w.wait()

    def project(k, carry):
        d = lax.rem(t + k, nt)
        cols = pl.ds(pl.multiple_of(width * d, width), width)
        p8 = jnp.dot(lhs, w[:, cols], preferred_element_type=jnp.float32)
        both = jnp.concatenate(
            [jnp.sum(p8[0:4], axis=0, keepdims=True), jnp.sum(p8[4:8], axis=0, keepdims=True)], axis=0
        )
        part[d] = both

        @pl.when(k < nt)
        def _():
            pltpu.make_async_remote_copy(
                src_ref=part.at[d],
                dst_ref=red.at[t],
                send_sem=red_sent,
                recv_sem=red_sem,
                device_id={"tensor": d},
                device_id_type=MESH,
            ).start()

        return carry

    lax.fori_loop(1, nt + 1, project, 0)
    red[t] = part[t]

    load_row_of.wait()
    wait_bytes(got.at[pl.ds(0, rows - 2)], hop1_sem)
    for_partners(0, nx // 4, hop2)

    wait_bytes(red.at[pl.ds(0, nt - 1)], red_sem)
    total = red[0]
    for i in range(1, nt):
        total = total + red[i]
    total = total + res_ref[0].astype(jnp.float32)
    lay_own[...] = total.astype(jnp.bfloat16)

    def hand(k, carry):
        pltpu.make_async_remote_copy(
            src_ref=lay_own,
            dst_ref=lay.at[g],
            send_sem=layz_sent,
            recv_sem=layz_sem,
            device_id={"group": x * nz + lax.rem(z + k, nz), "section": 1 - s},
            device_id_type=MESH,
        ).start()
        return carry

    lax.fori_loop(0, nz, hand, 0)

    for_partners(nx // 4, nx // 2, hop2)

    ring = pl.ds(nz * x, nz)
    wait_bytes(lay.at[pl.ds(0, nz)], layz_sem)

    def spread(k, carry):
        pltpu.make_async_remote_copy(
            src_ref=lay.at[ring],
            dst_ref=lay.at[ring],
            send_sem=layx_sent,
            recv_sem=layx_sem,
            device_id={"group": lax.rem(x + k, nx) * nz + z},
            device_id_type=MESH,
        ).start()
        return carry

    lax.fori_loop(1, nx, spread, 0)

    for_partners(nx // 2, nx, hop2)
    copy_slots(g)
    own = pltpu.make_async_copy(put.at[pl.ds(4 * g, 4)], cache_ref.at[0, :, :, mine, :], own_sem)
    own.start()

    wait_bytes(lay.at[pl.ds(0, nz * (nx - 1))], layx_sem)
    out_rows = []
    for slot in range(4):
        r = row_of_ref[0, 4 * g + slot]
        both = lay[jnp.minimum(r, rows - 1) // 2].astype(jnp.float32)
        out_rows.append(jnp.where(r < rows, jnp.where(r % 2 == 0, both[0:1], both[1:2]), 0.0))
    handed_ref[0] = jnp.concatenate(out_rows, axis=0).astype(jnp.bfloat16)

    wait_bytes(part.at[pl.ds(0, nt - 1)], red_sent)
    wait_bytes(lay.at[pl.ds(0, nz)], layz_sent)
    wait_bytes(lay.at[pl.ds(0, nz * (nx - 1))], layx_sent)
    wait_bytes(got.at[pl.ds(0, rows - 2)], sent_sem.at[0])
    own.wait()
    wait_bytes(put.at[pl.ds(0, 4 * (groups - 1))], sent_sem.at[1])
    wait_bytes(put.at[pl.ds(0, 4 * (groups - 1))], hop2_sem)


def write_kernel(handed, moved, handed_hbm, moved_hbm, sem):
    copies = [
        pltpu.make_async_copy(moved.at[0, i, c], moved_hbm.at[0, i, c], sem.at[2 * i + c])
        for i in range(4)
        for c in range(2)
    ]
    copies.append(pltpu.make_async_copy(handed, handed_hbm, sem.at[8]))
    for copy in copies:
        copy.start()
    for copy in copies:
        copy.wait()


def shards(nx, nz, nt, queries, kv_cache, new_kv, residual, out_weight, dest_cell, lengths):
    groups = nx * nz
    rows = 2 * groups
    cells = 4 * groups
    ctx = kv_cache.shape[3]
    span = ctx // groups
    width = residual.shape[-1]
    bf = jnp.bfloat16
    f32 = jnp.float32
    dma = pltpu.SemaphoreType.DMA
    vmem = pl.BlockSpec(memory_space=pltpu.VMEM)
    hbm = pl.BlockSpec(memory_space=pltpu.HBM)
    handed, moved = pl.pallas_call(
        functools.partial(move_kernel, nx, nz, nt),
        out_shape=(pltpu.VMEM((1, 4, width), bf), pltpu.VMEM((1, 4, 2, ctx, HD), bf)),
        in_specs=[hbm] * 7,
        out_specs=(vmem, vmem),
        scratch_shapes=[
            pltpu.SMEM((rows,), jnp.int32),
            pltpu.SMEM((rows,), jnp.int32),
            pltpu.VMEM(queries.shape, bf),
            pltpu.VMEM(new_kv.shape, bf),
            pltpu.VMEM(residual.shape, bf),
            pltpu.VMEM((8, cells), jnp.int32),
            pltpu.SMEM((8, cells), jnp.int32),
            pltpu.VMEM((2, 2, ctx, HD), bf),
            pltpu.VMEM(out_weight.shape[1:], bf),
            pltpu.VMEM((rows + 1, 2, span, HD), bf),
            pltpu.VMEM((cells, 2, span, HD), bf),
            pltpu.VMEM((nt, 2, width), f32),
            pltpu.VMEM((nt, 2, width), f32),
            pltpu.VMEM((2, width), bf),
            pltpu.VMEM((groups, 2, width), bf),
            dma, dma((5,)), dma, dma, dma, dma((2,)), dma, dma, dma, dma, dma, dma, dma, dma,
        ],
        compiler_params=pltpu.CompilerParams(
            collective_id=0, has_side_effects=True, vmem_limit_bytes=60 * 1024 * 1024
        ),
    )(dest_cell, lengths, queries, kv_cache, new_kv, residual, out_weight)
    return pl.pallas_call(
        write_kernel,
        out_shape=(
            jax.ShapeDtypeStruct(handed.shape, bf),
            jax.ShapeDtypeStruct(moved.shape, bf),
        ),
        in_specs=[vmem, vmem],
        out_specs=(hbm, hbm),
        scratch_shapes=[dma((9,))],
        compiler_params=pltpu.CompilerParams(vmem_limit_bytes=8 * 1024 * 1024),
    )(handed, moved)


def solution(mesh):
    in_specs = (
        P("section", "group", "tensor"),
        P("section", "group", None, None, "tensor"),
        P("section", "group", None, "tensor"),
        P("section", "group", "tensor"),
        P("section", "tensor", None),
        P(),
        P(),
    )
    out_specs = (P("section", "group", "tensor"), P("section", "group", None, None, "tensor"))
    nz = min(NZ, mesh.shape["group"] // 2)
    body = functools.partial(shards, mesh.shape["group"] // nz, nz, mesh.shape["tensor"])
    return jax.shard_map(body, mesh=mesh, in_specs=in_specs, out_specs=out_specs, check_vma=False)
```

```python
import functools

import jax
import jax.numpy as jnp
from jax import lax
from jax.experimental import pallas as pl
from jax.experimental.pallas import tpu as pltpu
from jax.sharding import PartitionSpec as P

HD = 128
NZ = 8
MESH = pl.DeviceIdType.MESH


def move_kernel(
    nx, nz, nt,
    dest_hbm, len_hbm, q_hbm, kv_hbm, fresh_hbm, res_hbm, w_hbm,
    handed_ref, cache_ref,
    dest_ref, len_ref, q_ref, fresh_ref, res_ref, row_of, row_of_ref,
    kv, w, got_k, got_v, put_k, put_v, part, red, lay_own, lay,
    in_sem, small_sem, row_sem, w_sem, own_sem, sent_sem, k1_sem, v1_sem, k2_sem, v2_sem, red_sent, red_sem, layz_sent, layx_sent, layz_sem, layx_sem,
):
    groups = nx * nz
    ctx = kv.shape[2]
    span = ctx // groups
    rows = 2 * groups
    g = lax.axis_index("group")
    s = lax.axis_index("section")
    t = lax.axis_index("tensor")
    x = lax.div(g, nz)
    z = lax.rem(g, nz)

    load_kv = [pltpu.make_async_copy(kv_hbm.at[0, :, c], kv.at[:, c], in_sem.at[c]) for c in range(2)]
    load_kv[0].start()
    small = [
        pltpu.make_async_copy(src, dst, small_sem.at[i])
        for i, (src, dst) in enumerate(
            ((len_hbm, len_ref), (fresh_hbm, fresh_ref), (q_hbm, q_ref), (dest_hbm, dest_ref), (res_hbm, res_ref))
        )
    ]
    load_len, load_fresh, *load_rest = small
    load_len.start()
    load_fresh.start()

    barrier = pltpu.get_barrier_semaphore()

    def greet_group(k, carry):
        pl.semaphore_signal(barrier, inc=1, device_id={"group": lax.rem(g + k, groups)}, device_id_type=MESH)
        return carry

    def greet_tensor(k, carry):
        pl.semaphore_signal(barrier, inc=1, device_id={"tensor": lax.rem(t + k, nt)}, device_id_type=MESH)
        return carry

    def greet_section(k, carry):
        pl.semaphore_signal(
            barrier, inc=1, device_id={"group": x * nz + lax.rem(z + k, nz), "section": 1 - s}, device_id_type=MESH
        )
        return carry

    lax.fori_loop(1, groups, greet_group, 0, unroll=True)
    lax.fori_loop(1, nt, greet_tensor, 0, unroll=True)
    lax.fori_loop(0, nz, greet_section, 0, unroll=True)

    for load in (load_kv[1], *load_rest):
        load.start()
    load_w = pltpu.make_async_copy(w_hbm.at[0], w, w_sem)
    load_w.start()

    load_len.wait()
    load_fresh.wait()
    len0 = len_ref[2 * g]
    len1 = len_ref[2 * g + 1]
    pos = lax.broadcasted_iota(jnp.int32, (ctx, HD), 0)
    mine = pl.ds(pl.multiple_of(span * g, span), span)

    def append(c, got):
        load_kv[c].wait()
        for r, n in ((0, len0), (1, len1)):
            token = jnp.broadcast_to(fresh_ref[0, r, c : c + 1, :].astype(jnp.float32), (ctx, HD))
            kv[r, c] = jnp.where(pos == n, token, kv[r, c].astype(jnp.float32)).astype(jnp.bfloat16)
            got[2 * g + r] = kv[r, c, mine, :]
        got[rows] = jnp.zeros((span, HD), jnp.bfloat16)

    append(0, got_k)
    pl.semaphore_wait(barrier, groups - 1 + nt - 1 + nz)

    z_offsets = [o for m in range(nz // 2 - 1, 0, -1) for o in (m, nz - m)]
    z_offsets[2:2] = [nz // 2]
    z_offsets.append(0)

    way = 1 - 2 * s

    later = z_offsets[nz // 2 :] + z_offsets[: nz // 2]
    z_partners = [lax.rem(z + jnp.where(s == 0, dz, nz - dz_later), nz) for dz, dz_later in zip(z_offsets, later)]

    def for_partners(low, high, send):
        def window(v, carry):
            for j in range(nz):
                d = lax.rem(x + way * (j + v) + nx * nz, nx) * nz + z_partners[j]
                if 0 in (z_offsets[j], later[j]):
                    pl.when(d != g)(functools.partial(send, d))
                else:
                    send(d)
            return carry

        lax.fori_loop(low, high, window, 0, unroll=True)

    def hop1(c, dst, sem, low, high):
        def send(d):
            pltpu.make_async_remote_copy(
                src_ref=kv.at[:, c, pl.ds(pl.multiple_of(span * d, span), span), :],
                dst_ref=dst.at[pl.ds(2 * g, 2)],
                send_sem=sent_sem.at[c],
                recv_sem=sem,
                device_id={"group": d},
                device_id_type=MESH,
            ).start()

        for_partners(low, high, send)

    hop1(0, got_k, k1_sem, 0, nx)
    append(1, got_v)
    hop1(1, got_v, v1_sem, 0, nx)

    for load in load_rest:
        load.wait()
    cells = row_of.shape[1]
    cell = lax.broadcasted_iota(jnp.int32, (8, cells), 1)

    def place(r, found):
        return jnp.where(cell == dest_ref[r], r, found)

    found = lax.fori_loop(0, rows, place, jnp.full((8, cells), rows, jnp.int32), unroll=8)
    row_of[...] = found
    load_row_of = pltpu.make_async_copy(row_of, row_of_ref, row_sem)
    load_row_of.start()

    qf = q_ref[0].astype(jnp.float32)
    q8 = jnp.concatenate(
        [qf[r : r + 1, h * HD : (h + 1) * HD] for r in range(2) for h in range(4)], axis=0
    ).astype(jnp.bfloat16)
    dims = (((1,), (1,)), ((), ()))
    first = lax.broadcasted_iota(jnp.int32, (8, ctx), 0) < 4
    scores = jnp.where(
        first,
        lax.dot_general(q8, kv[0, 0], dims, preferred_element_type=jnp.float32),
        lax.dot_general(q8, kv[1, 0], dims, preferred_element_type=jnp.float32),
    ) * (1.0 / HD**0.5)
    valid = lax.broadcasted_iota(jnp.int32, (8, ctx), 1) <= jnp.where(first, len0, len1)
    scores = jnp.where(valid, scores, -1e30)
    top = jnp.max(scores, axis=1, keepdims=True)
    e = jnp.where(valid, jnp.exp(scores - top), 0.0)
    weights = (e / jnp.sum(e, axis=1, keepdims=True)).astype(jnp.bfloat16)
    sub = lax.broadcasted_iota(jnp.int32, (8, HD), 0)
    attended = jnp.where(
        sub < 4,
        jnp.dot(weights, kv[0, 1], preferred_element_type=jnp.float32),
        jnp.dot(weights, kv[1, 1], preferred_element_type=jnp.float32),
    )
    lhs = jnp.concatenate(
        [jnp.where(sub % 4 == h, attended, 0.0) for h in range(4)], axis=1
    ).astype(jnp.bfloat16)

    def wait_bytes(ref, sem):
        pltpu.make_async_copy(ref, ref, sem).wait()

    def hop2(c, got, put, sem, low, high):
        def copy_slots(d):
            for slot in range(4):
                put[4 * d + slot] = got[row_of_ref[0, 4 * d + slot]]

        def send(d):
            copy_slots(d)
            pltpu.make_async_remote_copy(
                src_ref=put.at[pl.ds(4 * d, 4)],
                dst_ref=cache_ref.at[0, :, c, mine, :],
                send_sem=sent_sem.at[2 + c],
                recv_sem=sem,
                device_id={"group": d},
                device_id_type=MESH,
            ).start()

        for_partners(low, high, send)
        if high == nx:
            copy_slots(g)
            pltpu.make_async_copy(put.at[pl.ds(4 * g, 4)], cache_ref.at[0, :, c, mine, :], own_sem.at[c]).start()

    width = res_ref.shape[2]
    load_w.wait()

    def project(k, carry):
        d = lax.rem(t + k, nt)
        cols = pl.ds(pl.multiple_of(width * d, width), width)
        p8 = jnp.dot(lhs, w[:, cols], preferred_element_type=jnp.float32)
        both = jnp.concatenate(
            [jnp.sum(p8[0:4], axis=0, keepdims=True), jnp.sum(p8[4:8], axis=0, keepdims=True)], axis=0
        )
        part[d] = both

        @pl.when(k < nt)
        def _():
            pltpu.make_async_remote_copy(
                src_ref=part.at[d],
                dst_ref=red.at[t],
                send_sem=red_sent,
                recv_sem=red_sem,
                device_id={"tensor": d},
                device_id_type=MESH,
            ).start()

        return carry

    lax.fori_loop(1, nt + 1, project, 0)
    red[t] = part[t]

    load_row_of.wait()
    wait_bytes(got_k.at[pl.ds(0, rows - 2)], k1_sem)
    hop2(0, got_k, put_k, k2_sem, 0, nx // 2)

    wait_bytes(red.at[pl.ds(0, nt - 1)], red_sem)
    total = red[0]
    for i in range(1, nt):
        total = total + red[i]
    total = total + res_ref[0].astype(jnp.float32)
    lay_own[...] = total.astype(jnp.bfloat16)

    def hand(k, carry):
        pltpu.make_async_remote_copy(
            src_ref=lay_own,
            dst_ref=lay.at[g],
            send_sem=layz_sent,
            recv_sem=layz_sem,
            device_id={"group": x * nz + lax.rem(z + k, nz), "section": 1 - s},
            device_id_type=MESH,
        ).start()
        return carry

    lax.fori_loop(0, nz, hand, 0, unroll=True)

    hop2(0, got_k, put_k, k2_sem, nx // 2, nx)

    ring = pl.ds(nz * x, nz)
    wait_bytes(lay.at[pl.ds(0, nz)], layz_sem)

    def spread(k, carry):
        pltpu.make_async_remote_copy(
            src_ref=lay.at[ring],
            dst_ref=lay.at[ring],
            send_sem=layx_sent,
            recv_sem=layx_sem,
            device_id={"group": lax.rem(x + k, nx) * nz + z},
            device_id_type=MESH,
        ).start()
        return carry

    lax.fori_loop(1, nx, spread, 0, unroll=True)

    wait_bytes(got_v.at[pl.ds(0, rows - 2)], v1_sem)
    hop2(1, got_v, put_v, v2_sem, 0, nx)

    wait_bytes(lay.at[pl.ds(0, nz * (nx - 1))], layx_sem)
    out_rows = []
    for slot in range(4):
        r = row_of_ref[0, 4 * g + slot]
        both = lay[jnp.minimum(r, rows - 1) // 2].astype(jnp.float32)
        out_rows.append(jnp.where(r < rows, jnp.where(r % 2 == 0, both[0:1], both[1:2]), 0.0))
    handed_ref[0] = jnp.concatenate(out_rows, axis=0).astype(jnp.bfloat16)

    wait_bytes(part.at[pl.ds(0, nt - 1)], red_sent)
    wait_bytes(lay.at[pl.ds(0, nz)], layz_sent)
    wait_bytes(lay.at[pl.ds(0, nz * (nx - 1))], layx_sent)
    wait_bytes(got_k.at[pl.ds(0, rows - 2)], sent_sem.at[0])
    wait_bytes(got_v.at[pl.ds(0, rows - 2)], sent_sem.at[1])
    for c, put, sem in ((0, put_k, k2_sem), (1, put_v, v2_sem)):
        pltpu.make_async_copy(put.at[pl.ds(4 * g, 4)], cache_ref.at[0, :, c, mine, :], own_sem.at[c]).wait()
        wait_bytes(put.at[pl.ds(0, 4 * (groups - 1))], sent_sem.at[2 + c])
        wait_bytes(put.at[pl.ds(0, 4 * (groups - 1))], sem)


def write_kernel(handed, moved, handed_hbm, moved_hbm, sem):
    copies = [
        pltpu.make_async_copy(moved.at[0, i, c], moved_hbm.at[0, i, c], sem.at[2 * i + c])
        for i in range(4)
        for c in range(2)
    ]
    copies.append(pltpu.make_async_copy(handed, handed_hbm, sem.at[8]))
    for copy in copies:
        copy.start()
    for copy in copies:
        copy.wait()


def shards(nx, nz, nt, queries, kv_cache, new_kv, residual, out_weight, dest_cell, lengths):
    groups = nx * nz
    rows = 2 * groups
    cells = 4 * groups
    ctx = kv_cache.shape[3]
    span = ctx // groups
    width = residual.shape[-1]
    bf = jnp.bfloat16
    f32 = jnp.float32
    dma = pltpu.SemaphoreType.DMA
    vmem = pl.BlockSpec(memory_space=pltpu.VMEM)
    hbm = pl.BlockSpec(memory_space=pltpu.HBM)
    handed, moved = pl.pallas_call(
        functools.partial(move_kernel, nx, nz, nt),
        out_shape=(pltpu.VMEM((1, 4, width), bf), pltpu.VMEM((1, 4, 2, ctx, HD), bf)),
        in_specs=[hbm] * 7,
        out_specs=(vmem, vmem),
        scratch_shapes=[
            pltpu.SMEM((rows,), jnp.int32),
            pltpu.SMEM((rows,), jnp.int32),
            pltpu.VMEM(queries.shape, bf),
            pltpu.VMEM(new_kv.shape, bf),
            pltpu.VMEM(residual.shape, bf),
            pltpu.VMEM((8, cells), jnp.int32),
            pltpu.SMEM((8, cells), jnp.int32),
            pltpu.VMEM((2, 2, ctx, HD), bf),
            pltpu.VMEM(out_weight.shape[1:], bf),
            pltpu.VMEM((rows + 1, span, HD), bf),
            pltpu.VMEM((rows + 1, span, HD), bf),
            pltpu.VMEM((cells, span, HD), bf),
            pltpu.VMEM((cells, span, HD), bf),
            pltpu.VMEM((nt, 2, width), f32),
            pltpu.VMEM((nt, 2, width), f32),
            pltpu.VMEM((2, width), bf),
            pltpu.VMEM((groups, 2, width), bf),
            dma((2,)), dma((5,)), dma, dma, dma((2,)), dma((4,)), dma, dma, dma, dma, dma, dma, dma, dma, dma, dma,
        ],
        compiler_params=pltpu.CompilerParams(
            collective_id=0, has_side_effects=True, vmem_limit_bytes=60 * 1024 * 1024
        ),
    )(dest_cell, lengths, queries, kv_cache, new_kv, residual, out_weight)
    return pl.pallas_call(
        write_kernel,
        out_shape=(
            jax.ShapeDtypeStruct(handed.shape, bf),
            jax.ShapeDtypeStruct(moved.shape, bf),
        ),
        in_specs=[vmem, vmem],
        out_specs=(hbm, hbm),
        scratch_shapes=[dma((9,))],
        compiler_params=pltpu.CompilerParams(vmem_limit_bytes=8 * 1024 * 1024),
    )(handed, moved)


def solution(mesh):
    in_specs = (
        P("section", "group", "tensor"),
        P("section", "group", None, None, "tensor"),
        P("section", "group", None, "tensor"),
        P("section", "group", "tensor"),
        P("section", "tensor", None),
        P(),
        P(),
    )
    out_specs = (P("section", "group", "tensor"), P("section", "group", None, None, "tensor"))
    nz = min(NZ, mesh.shape["group"] // 2)
    body = functools.partial(shards, mesh.shape["group"] // nz, nz, mesh.shape["tensor"])
    return jax.shard_map(body, mesh=mesh, in_specs=in_specs, out_specs=out_specs, check_vma=False)
```

```python
import functools

import jax
import jax.numpy as jnp
from jax import lax
from jax.experimental import pallas as pl
from jax.experimental.pallas import tpu as pltpu
from jax.sharding import PartitionSpec as P

HD = 128
NZ = 8
MESH = pl.DeviceIdType.MESH


def move_kernel(
    nx, nz, nt,
    dest_hbm, len_hbm, q_hbm, kv_hbm, fresh_hbm, res_hbm, w_hbm,
    handed_ref, cache_ref,
    dest_ref, len_ref, q_ref, fresh_ref, res_ref, row_of, row_of_ref,
    kv, w, got_k, got_v, put_k, put_v, part, red, lay_own, lay,
    in_sem, small_sem, row_sem, w_sem, own_sem, sent_sem, k1_sem, v1_sem, k2_sem, v2_sem, red_sent, red_sem, layz_sent, layx_sent, layz_sem, layx_sem,
):
    groups = nx * nz
    ctx = kv.shape[2]
    span = ctx // groups
    rows = 2 * groups
    g = lax.axis_index("group")
    s = lax.axis_index("section")
    t = lax.axis_index("tensor")
    x = lax.div(g, nz)
    z = lax.rem(g, nz)

    load_kv = [pltpu.make_async_copy(kv_hbm.at[0, :, c], kv.at[:, c], in_sem.at[c]) for c in range(2)]
    load_kv[0].start()
    small = [
        pltpu.make_async_copy(src, dst, small_sem.at[i])
        for i, (src, dst) in enumerate(
            ((len_hbm, len_ref), (fresh_hbm, fresh_ref), (q_hbm, q_ref), (dest_hbm, dest_ref), (res_hbm, res_ref))
        )
    ]
    load_len, load_fresh, *load_rest = small
    load_len.start()
    load_fresh.start()

    barrier = pltpu.get_barrier_semaphore()

    def greet_group(k, carry):
        pl.semaphore_signal(barrier, inc=1, device_id={"group": lax.rem(g + k, groups)}, device_id_type=MESH)
        return carry

    def greet_tensor(k, carry):
        pl.semaphore_signal(barrier, inc=1, device_id={"tensor": lax.rem(t + k, nt)}, device_id_type=MESH)
        return carry

    def greet_section(k, carry):
        pl.semaphore_signal(
            barrier, inc=1, device_id={"group": x * nz + lax.rem(z + k, nz), "section": 1 - s}, device_id_type=MESH
        )
        return carry

    lax.fori_loop(1, groups, greet_group, 0, unroll=True)
    lax.fori_loop(1, nt, greet_tensor, 0, unroll=True)
    lax.fori_loop(0, nz, greet_section, 0, unroll=True)

    for load in (load_kv[1], *load_rest):
        load.start()
    load_w = pltpu.make_async_copy(w_hbm.at[0], w, w_sem)
    load_w.start()

    load_len.wait()
    load_fresh.wait()
    len0 = len_ref[2 * g]
    len1 = len_ref[2 * g + 1]
    pos = lax.broadcasted_iota(jnp.int32, (ctx, HD), 0)
    mine = pl.ds(pl.multiple_of(span * g, span), span)

    def append(c, got):
        load_kv[c].wait()
        for r, n in ((0, len0), (1, len1)):
            token = jnp.broadcast_to(fresh_ref[0, r, c : c + 1, :].astype(jnp.float32), (ctx, HD))
            kv[r, c] = jnp.where(pos == n, token, kv[r, c].astype(jnp.float32)).astype(jnp.bfloat16)
            got[2 * g + r] = kv[r, c, mine, :]
        got[rows] = jnp.zeros((span, HD), jnp.bfloat16)

    append(0, got_k)
    pl.semaphore_wait(barrier, groups - 1 + nt - 1 + nz)

    z_offsets = [o for m in range(nz // 2 - 1, 0, -1) for o in (m, nz - m)]
    z_offsets[2:2] = [nz // 2]
    z_offsets.append(0)

    way = 1 - 2 * s

    odd = lax.rem(x, 2)
    z_partners = []
    may_be_own = []
    for j in range(nz):
        even_0, odd_0, even_1, odd_1 = (z_offsets[(j + i * nz // 4) % nz] for i in range(4))
        ahead = jnp.where(odd == 0, even_0, odd_0)
        behind = nz - jnp.where(odd == 0, even_1, odd_1)
        z_partners.append(lax.rem(z + jnp.where(s == 0, ahead, behind), nz))
        may_be_own.append(0 in (even_0, odd_0, even_1, odd_1))

    def for_partners(low, high, send):
        def window(v, carry):
            for j in range(nz):
                d = lax.rem(x + way * (j + v) + nx * nz, nx) * nz + z_partners[j]
                if may_be_own[j]:
                    pl.when(d != g)(functools.partial(send, d))
                else:
                    send(d)
            return carry

        lax.fori_loop(low, high, window, 0, unroll=True)

    def hop1(c, dst, sem, low, high):
        def send(d):
            pltpu.make_async_remote_copy(
                src_ref=kv.at[:, c, pl.ds(pl.multiple_of(span * d, span), span), :],
                dst_ref=dst.at[pl.ds(2 * g, 2)],
                send_sem=sent_sem.at[c],
                recv_sem=sem,
                device_id={"group": d},
                device_id_type=MESH,
            ).start()

        for_partners(low, high, send)

    hop1(0, got_k, k1_sem, 0, nx)
    append(1, got_v)
    hop1(1, got_v, v1_sem, 0, nx)

    for load in load_rest:
        load.wait()
    cells = row_of.shape[1]
    cell = lax.broadcasted_iota(jnp.int32, (8, cells), 1)

    def place(r, found):
        return jnp.where(cell == dest_ref[r], r, found)

    found = lax.fori_loop(0, rows, place, jnp.full((8, cells), rows, jnp.int32), unroll=8)
    row_of[...] = found
    load_row_of = pltpu.make_async_copy(row_of, row_of_ref, row_sem)
    load_row_of.start()

    qf = q_ref[0].astype(jnp.float32)
    q8 = jnp.concatenate(
        [qf[r : r + 1, h * HD : (h + 1) * HD] for r in range(2) for h in range(4)], axis=0
    ).astype(jnp.bfloat16)
    dims = (((1,), (1,)), ((), ()))
    first = lax.broadcasted_iota(jnp.int32, (8, ctx), 0) < 4
    scores = jnp.where(
        first,
        lax.dot_general(q8, kv[0, 0], dims, preferred_element_type=jnp.float32),
        lax.dot_general(q8, kv[1, 0], dims, preferred_element_type=jnp.float32),
    ) * (1.0 / HD**0.5)
    valid = lax.broadcasted_iota(jnp.int32, (8, ctx), 1) <= jnp.where(first, len0, len1)
    scores = jnp.where(valid, scores, -1e30)
    top = jnp.max(scores, axis=1, keepdims=True)
    e = jnp.where(valid, jnp.exp(scores - top), 0.0)
    weights = (e / jnp.sum(e, axis=1, keepdims=True)).astype(jnp.bfloat16)
    sub = lax.broadcasted_iota(jnp.int32, (8, HD), 0)
    attended = jnp.where(
        sub < 4,
        jnp.dot(weights, kv[0, 1], preferred_element_type=jnp.float32),
        jnp.dot(weights, kv[1, 1], preferred_element_type=jnp.float32),
    )
    lhs = jnp.concatenate(
        [jnp.where(sub % 4 == h, attended, 0.0) for h in range(4)], axis=1
    ).astype(jnp.bfloat16)

    def wait_bytes(ref, sem):
        pltpu.make_async_copy(ref, ref, sem).wait()

    def hop2(c, got, put, sem, low, high):
        def copy_slots(d):
            for slot in range(4):
                put[4 * d + slot] = got[row_of_ref[0, 4 * d + slot]]

        def send(d):
            copy_slots(d)
            pltpu.make_async_remote_copy(
                src_ref=put.at[pl.ds(4 * d, 4)],
                dst_ref=cache_ref.at[0, :, c, mine, :],
                send_sem=sent_sem.at[2 + c],
                recv_sem=sem,
                device_id={"group": d},
                device_id_type=MESH,
            ).start()

        for_partners(low, high, send)
        if high == nx:
            copy_slots(g)
            pltpu.make_async_copy(put.at[pl.ds(4 * g, 4)], cache_ref.at[0, :, c, mine, :], own_sem.at[c]).start()

    width = res_ref.shape[2]
    load_w.wait()

    def project(k, carry):
        d = lax.rem(t + k, nt)
        cols = pl.ds(pl.multiple_of(width * d, width), width)
        p8 = jnp.dot(lhs, w[:, cols], preferred_element_type=jnp.float32)
        both = jnp.concatenate(
            [jnp.sum(p8[0:4], axis=0, keepdims=True), jnp.sum(p8[4:8], axis=0, keepdims=True)], axis=0
        )
        part[d] = both

        @pl.when(k < nt)
        def _():
            pltpu.make_async_remote_copy(
                src_ref=part.at[d],
                dst_ref=red.at[t],
                send_sem=red_sent,
                recv_sem=red_sem,
                device_id={"tensor": d},
                device_id_type=MESH,
            ).start()

        return carry

    lax.fori_loop(1, nt + 1, project, 0)
    red[t] = part[t]

    load_row_of.wait()
    wait_bytes(got_k.at[pl.ds(0, rows - 2)], k1_sem)
    hop2(0, got_k, put_k, k2_sem, 0, nx // 2)

    wait_bytes(red.at[pl.ds(0, nt - 1)], red_sem)
    total = red[0]
    for i in range(1, nt):
        total = total + red[i]
    total = total + res_ref[0].astype(jnp.float32)
    lay_own[...] = total.astype(jnp.bfloat16)

    def hand(k, carry):
        pltpu.make_async_remote_copy(
            src_ref=lay_own,
            dst_ref=lay.at[g],
            send_sem=layz_sent,
            recv_sem=layz_sem,
            device_id={"group": x * nz + lax.rem(z + k, nz), "section": 1 - s},
            device_id_type=MESH,
        ).start()
        return carry

    lax.fori_loop(0, nz, hand, 0, unroll=True)

    hop2(0, got_k, put_k, k2_sem, nx // 2, nx)

    ring = pl.ds(nz * x, nz)
    wait_bytes(lay.at[pl.ds(0, nz)], layz_sem)

    def spread(k, carry):
        pltpu.make_async_remote_copy(
            src_ref=lay.at[ring],
            dst_ref=lay.at[ring],
            send_sem=layx_sent,
            recv_sem=layx_sem,
            device_id={"group": lax.rem(x + k, nx) * nz + z},
            device_id_type=MESH,
        ).start()
        return carry

    lax.fori_loop(1, nx, spread, 0, unroll=True)

    wait_bytes(got_v.at[pl.ds(0, rows - 2)], v1_sem)
    hop2(1, got_v, put_v, v2_sem, 0, nx)

    wait_bytes(lay.at[pl.ds(0, nz * (nx - 1))], layx_sem)
    out_rows = []
    for slot in range(4):
        r = row_of_ref[0, 4 * g + slot]
        both = lay[jnp.minimum(r, rows - 1) // 2].astype(jnp.float32)
        out_rows.append(jnp.where(r < rows, jnp.where(r % 2 == 0, both[0:1], both[1:2]), 0.0))
    handed_ref[0] = jnp.concatenate(out_rows, axis=0).astype(jnp.bfloat16)

    wait_bytes(part.at[pl.ds(0, nt - 1)], red_sent)
    wait_bytes(lay.at[pl.ds(0, nz)], layz_sent)
    wait_bytes(lay.at[pl.ds(0, nz * (nx - 1))], layx_sent)
    wait_bytes(got_k.at[pl.ds(0, rows - 2)], sent_sem.at[0])
    wait_bytes(got_v.at[pl.ds(0, rows - 2)], sent_sem.at[1])
    for c, put, sem in ((0, put_k, k2_sem), (1, put_v, v2_sem)):
        pltpu.make_async_copy(put.at[pl.ds(4 * g, 4)], cache_ref.at[0, :, c, mine, :], own_sem.at[c]).wait()
        wait_bytes(put.at[pl.ds(0, 4 * (groups - 1))], sent_sem.at[2 + c])
        wait_bytes(put.at[pl.ds(0, 4 * (groups - 1))], sem)


def write_kernel(handed, moved, handed_hbm, moved_hbm, sem):
    copies = [
        pltpu.make_async_copy(moved.at[0, i, c], moved_hbm.at[0, i, c], sem.at[2 * i + c])
        for i in range(4)
        for c in range(2)
    ]
    copies.append(pltpu.make_async_copy(handed, handed_hbm, sem.at[8]))
    for copy in copies:
        copy.start()
    for copy in copies:
        copy.wait()


def shards(nx, nz, nt, queries, kv_cache, new_kv, residual, out_weight, dest_cell, lengths):
    groups = nx * nz
    rows = 2 * groups
    cells = 4 * groups
    ctx = kv_cache.shape[3]
    span = ctx // groups
    width = residual.shape[-1]
    bf = jnp.bfloat16
    f32 = jnp.float32
    dma = pltpu.SemaphoreType.DMA
    vmem = pl.BlockSpec(memory_space=pltpu.VMEM)
    hbm = pl.BlockSpec(memory_space=pltpu.HBM)
    handed, moved = pl.pallas_call(
        functools.partial(move_kernel, nx, nz, nt),
        out_shape=(pltpu.VMEM((1, 4, width), bf), pltpu.VMEM((1, 4, 2, ctx, HD), bf)),
        in_specs=[hbm] * 7,
        out_specs=(vmem, vmem),
        scratch_shapes=[
            pltpu.SMEM((rows,), jnp.int32),
            pltpu.SMEM((rows,), jnp.int32),
            pltpu.VMEM(queries.shape, bf),
            pltpu.VMEM(new_kv.shape, bf),
            pltpu.VMEM(residual.shape, bf),
            pltpu.VMEM((8, cells), jnp.int32),
            pltpu.SMEM((8, cells), jnp.int32),
            pltpu.VMEM((2, 2, ctx, HD), bf),
            pltpu.VMEM(out_weight.shape[1:], bf),
            pltpu.VMEM((rows + 1, span, HD), bf),
            pltpu.VMEM((rows + 1, span, HD), bf),
            pltpu.VMEM((cells, span, HD), bf),
            pltpu.VMEM((cells, span, HD), bf),
            pltpu.VMEM((nt, 2, width), f32),
            pltpu.VMEM((nt, 2, width), f32),
            pltpu.VMEM((2, width), bf),
            pltpu.VMEM((groups, 2, width), bf),
            dma((2,)), dma((5,)), dma, dma, dma((2,)), dma((4,)), dma, dma, dma, dma, dma, dma, dma, dma, dma, dma,
        ],
        compiler_params=pltpu.CompilerParams(
            collective_id=0, has_side_effects=True, vmem_limit_bytes=60 * 1024 * 1024
        ),
    )(dest_cell, lengths, queries, kv_cache, new_kv, residual, out_weight)
    return pl.pallas_call(
        write_kernel,
        out_shape=(
            jax.ShapeDtypeStruct(handed.shape, bf),
            jax.ShapeDtypeStruct(moved.shape, bf),
        ),
        in_specs=[vmem, vmem],
        out_specs=(hbm, hbm),
        scratch_shapes=[dma((9,))],
        compiler_params=pltpu.CompilerParams(vmem_limit_bytes=8 * 1024 * 1024),
    )(handed, moved)


def solution(mesh):
    in_specs = (
        P("section", "group", "tensor"),
        P("section", "group", None, None, "tensor"),
        P("section", "group", None, "tensor"),
        P("section", "group", "tensor"),
        P("section", "tensor", None),
        P(),
        P(),
    )
    out_specs = (P("section", "group", "tensor"), P("section", "group", None, None, "tensor"))
    nz = min(NZ, mesh.shape["group"] // 2)
    body = functools.partial(shards, mesh.shape["group"] // nz, nz, mesh.shape["tensor"])
    return jax.shard_map(body, mesh=mesh, in_specs=in_specs, out_specs=out_specs, check_vma=False)
```

```python
import functools

import jax
import jax.numpy as jnp
from jax import lax
from jax.experimental import pallas as pl
from jax.experimental.pallas import tpu as pltpu
from jax.sharding import PartitionSpec as P

HD = 128
NZ = 8
MESH = pl.DeviceIdType.MESH


def move_kernel(
    nx, nz, nt,
    dest_hbm, len_hbm, q_hbm, kv_hbm, fresh_hbm, res_hbm, w_hbm,
    handed_ref, cache_ref,
    dest_ref, len_ref, q_ref, fresh_ref, res_ref, row_of, row_of_ref,
    kv, w, got_k, got_v, put_k, put_v, part, red, lay_own, lay,
    in_sem, small_sem, row_sem, w_sem, own_sem, sent_sem, k1_sem, v1_sem, k2_sem, v2_sem, red_sent, red_sem, layz_sent, layx_sent, layz_sem, layx_sem,
):
    groups = nx * nz
    ctx = kv.shape[2]
    span = ctx // groups
    rows = 2 * groups
    g = lax.axis_index("group")
    s = lax.axis_index("section")
    t = lax.axis_index("tensor")
    x = lax.div(g, nz)
    z = lax.rem(g, nz)

    load_kv = [pltpu.make_async_copy(kv_hbm.at[0, :, c], kv.at[:, c], in_sem.at[c]) for c in range(2)]
    load_kv[0].start()
    small = [
        pltpu.make_async_copy(src, dst, small_sem.at[i])
        for i, (src, dst) in enumerate(
            ((len_hbm, len_ref), (fresh_hbm, fresh_ref), (q_hbm, q_ref), (dest_hbm, dest_ref), (res_hbm, res_ref))
        )
    ]
    load_len, load_fresh, *load_rest = small
    load_len.start()
    load_fresh.start()

    barrier = pltpu.get_barrier_semaphore()

    def greet_group(k, carry):
        pl.semaphore_signal(barrier, inc=1, device_id={"group": lax.rem(g + k, groups)}, device_id_type=MESH)
        return carry

    def greet_tensor(k, carry):
        pl.semaphore_signal(barrier, inc=1, device_id={"tensor": lax.rem(t + k, nt)}, device_id_type=MESH)
        return carry

    def greet_section(k, carry):
        pl.semaphore_signal(
            barrier, inc=1, device_id={"group": x * nz + lax.rem(z + k, nz), "section": 1 - s}, device_id_type=MESH
        )
        return carry

    lax.fori_loop(1, groups, greet_group, 0, unroll=True)
    lax.fori_loop(1, nt, greet_tensor, 0, unroll=True)
    lax.fori_loop(0, nz, greet_section, 0, unroll=True)

    for load in (load_kv[1], *load_rest):
        load.start()
    load_w = pltpu.make_async_copy(w_hbm.at[0], w, w_sem)
    load_w.start()

    load_len.wait()
    load_fresh.wait()
    len0 = len_ref[2 * g]
    len1 = len_ref[2 * g + 1]
    pos = lax.broadcasted_iota(jnp.int32, (ctx, HD), 0)
    mine = pl.ds(pl.multiple_of(span * g, span), span)

    def append(c, got):
        load_kv[c].wait()
        for r, n in ((0, len0), (1, len1)):
            token = jnp.broadcast_to(fresh_ref[0, r, c : c + 1, :].astype(jnp.float32), (ctx, HD))
            kv[r, c] = jnp.where(pos == n, token, kv[r, c].astype(jnp.float32)).astype(jnp.bfloat16)
            got[2 * g + r] = kv[r, c, mine, :]
        got[rows] = jnp.zeros((span, HD), jnp.bfloat16)

    append(0, got_k)
    pl.semaphore_wait(barrier, groups - 1 + nt - 1 + nz)

    z_offsets = [o for m in range(nz // 2 - 1, 0, -1) for o in (m, nz - m)]
    z_offsets[2:2] = [nz // 2]
    z_offsets.append(0)

    way = 1 - 2 * s

    later = z_offsets[nz // 2 :] + z_offsets[: nz // 2]
    z_partners = [lax.rem(z + jnp.where(s == 0, dz, nz - dz_later), nz) for dz, dz_later in zip(z_offsets, later)]

    def for_partners(low, high, send):
        def window(v, carry):
            for j in range(nz):
                d = lax.rem(x + way * (j + v) + nx * nz, nx) * nz + z_partners[j]
                if 0 in (z_offsets[j], later[j]):
                    pl.when(d != g)(functools.partial(send, d))
                else:
                    send(d)
            return carry

        lax.fori_loop(low, high, window, 0, unroll=True)

    def hop1(c, dst, sem, low, high):
        def send(d):
            pltpu.make_async_remote_copy(
                src_ref=kv.at[:, c, pl.ds(pl.multiple_of(span * d, span), span), :],
                dst_ref=dst.at[pl.ds(2 * g, 2)],
                send_sem=sent_sem.at[c],
                recv_sem=sem,
                device_id={"group": d},
                device_id_type=MESH,
            ).start()

        for_partners(low, high, send)

    hop1(0, got_k, k1_sem, 0, nx)
    append(1, got_v)
    hop1(1, got_v, v1_sem, 0, nx)

    for load in load_rest:
        load.wait()
    cells = row_of.shape[1]
    cell = lax.broadcasted_iota(jnp.int32, (8, cells), 1)

    def place(r, found):
        return jnp.where(cell == dest_ref[r], r, found)

    found = lax.fori_loop(0, rows, place, jnp.full((8, cells), rows, jnp.int32), unroll=8)
    row_of[...] = found
    load_row_of = pltpu.make_async_copy(row_of, row_of_ref, row_sem)
    load_row_of.start()

    qf = q_ref[0].astype(jnp.float32)
    q8 = jnp.concatenate(
        [qf[r : r + 1, h * HD : (h + 1) * HD] for r in range(2) for h in range(4)], axis=0
    ).astype(jnp.bfloat16)
    dims = (((1,), (1,)), ((), ()))
    first = lax.broadcasted_iota(jnp.int32, (8, ctx), 0) < 4
    scores = jnp.where(
        first,
        lax.dot_general(q8, kv[0, 0], dims, preferred_element_type=jnp.float32),
        lax.dot_general(q8, kv[1, 0], dims, preferred_element_type=jnp.float32),
    ) * (1.0 / HD**0.5)
    valid = lax.broadcasted_iota(jnp.int32, (8, ctx), 1) <= jnp.where(first, len0, len1)
    scores = jnp.where(valid, scores, -1e30)
    top = jnp.max(scores, axis=1, keepdims=True)
    e = jnp.where(valid, jnp.exp(scores - top), 0.0)
    weights = (e / jnp.sum(e, axis=1, keepdims=True)).astype(jnp.bfloat16)
    sub = lax.broadcasted_iota(jnp.int32, (8, HD), 0)
    attended = jnp.where(
        sub < 4,
        jnp.dot(weights, kv[0, 1], preferred_element_type=jnp.float32),
        jnp.dot(weights, kv[1, 1], preferred_element_type=jnp.float32),
    )
    lhs = jnp.concatenate(
        [jnp.where(sub % 4 == h, attended, 0.0) for h in range(4)], axis=1
    ).astype(jnp.bfloat16)

    def wait_bytes(ref, sem):
        pltpu.make_async_copy(ref, ref, sem).wait()

    def hop2(c, got, put, sem, low, high):
        def copy_slots(d):
            for slot in range(4):
                put[4 * d + slot] = got[row_of_ref[0, 4 * d + slot]]

        def send(d):
            copy_slots(d)
            pltpu.make_async_remote_copy(
                src_ref=put.at[pl.ds(4 * d, 4)],
                dst_ref=cache_ref.at[0, :, c, mine, :],
                send_sem=sent_sem.at[2 + c],
                recv_sem=sem,
                device_id={"group": d},
                device_id_type=MESH,
            ).start()

        for_partners(low, high, send)
        if high == nx:
            copy_slots(g)
            pltpu.make_async_copy(put.at[pl.ds(4 * g, 4)], cache_ref.at[0, :, c, mine, :], own_sem.at[c]).start()

    width = res_ref.shape[2]
    load_w.wait()

    def project(k, carry):
        d = lax.rem(t + k, nt)
        cols = pl.ds(pl.multiple_of(width * d, width), width)
        p8 = jnp.dot(lhs, w[:, cols], preferred_element_type=jnp.float32)
        both = jnp.concatenate(
            [jnp.sum(p8[0:4], axis=0, keepdims=True), jnp.sum(p8[4:8], axis=0, keepdims=True)], axis=0
        )
        part[d] = both

        @pl.when(k < nt)
        def _():
            pltpu.make_async_remote_copy(
                src_ref=part.at[d],
                dst_ref=red.at[t],
                send_sem=red_sent,
                recv_sem=red_sem,
                device_id={"tensor": d},
                device_id_type=MESH,
            ).start()

        return carry

    lax.fori_loop(1, nt + 1, project, 0)
    red[t] = part[t]

    load_row_of.wait()
    wait_bytes(got_k.at[pl.ds(0, rows - 2)], k1_sem)
    hop2(0, got_k, put_k, k2_sem, 0, nx // 2)

    wait_bytes(red.at[pl.ds(0, nt - 1)], red_sem)
    total = red[0]
    for i in range(1, nt):
        total = total + red[i]
    total = total + res_ref[0].astype(jnp.float32)
    lay_own[...] = total.astype(jnp.bfloat16)

    def hand(k, carry):
        pltpu.make_async_remote_copy(
            src_ref=lay_own,
            dst_ref=lay.at[g],
            send_sem=layz_sent,
            recv_sem=layz_sem,
            device_id={"group": x * nz + lax.rem(z + k, nz), "section": 1 - s},
            device_id_type=MESH,
        ).start()
        return carry

    lax.fori_loop(0, nz, hand, 0, unroll=True)

    hop2(0, got_k, put_k, k2_sem, nx // 2, nx)

    wait_bytes(got_v.at[pl.ds(0, rows - 2)], v1_sem)
    hop2(1, got_v, put_v, v2_sem, 0, nx // 2)

    ring = pl.ds(nz * x, nz)
    wait_bytes(lay.at[pl.ds(0, nz)], layz_sem)

    def spread(k, carry):
        pltpu.make_async_remote_copy(
            src_ref=lay.at[ring],
            dst_ref=lay.at[ring],
            send_sem=layx_sent,
            recv_sem=layx_sem,
            device_id={"group": lax.rem(x + k, nx) * nz + z},
            device_id_type=MESH,
        ).start()
        return carry

    lax.fori_loop(1, nx, spread, 0, unroll=True)

    hop2(1, got_v, put_v, v2_sem, nx // 2, nx)

    wait_bytes(lay.at[pl.ds(0, nz * (nx - 1))], layx_sem)
    out_rows = []
    for slot in range(4):
        r = row_of_ref[0, 4 * g + slot]
        both = lay[jnp.minimum(r, rows - 1) // 2].astype(jnp.float32)
        out_rows.append(jnp.where(r < rows, jnp.where(r % 2 == 0, both[0:1], both[1:2]), 0.0))
    handed_ref[0] = jnp.concatenate(out_rows, axis=0).astype(jnp.bfloat16)

    wait_bytes(part.at[pl.ds(0, nt - 1)], red_sent)
    wait_bytes(lay.at[pl.ds(0, nz)], layz_sent)
    wait_bytes(lay.at[pl.ds(0, nz * (nx - 1))], layx_sent)
    wait_bytes(got_k.at[pl.ds(0, rows - 2)], sent_sem.at[0])
    wait_bytes(got_v.at[pl.ds(0, rows - 2)], sent_sem.at[1])
    for c, put, sem in ((0, put_k, k2_sem), (1, put_v, v2_sem)):
        pltpu.make_async_copy(put.at[pl.ds(4 * g, 4)], cache_ref.at[0, :, c, mine, :], own_sem.at[c]).wait()
        wait_bytes(put.at[pl.ds(0, 4 * (groups - 1))], sent_sem.at[2 + c])
        wait_bytes(put.at[pl.ds(0, 4 * (groups - 1))], sem)


def write_kernel(handed, moved, handed_hbm, moved_hbm, sem):
    copies = [
        pltpu.make_async_copy(moved.at[0, i, c], moved_hbm.at[0, i, c], sem.at[2 * i + c])
        for i in range(4)
        for c in range(2)
    ]
    copies.append(pltpu.make_async_copy(handed, handed_hbm, sem.at[8]))
    for copy in copies:
        copy.start()
    for copy in copies:
        copy.wait()


def shards(nx, nz, nt, queries, kv_cache, new_kv, residual, out_weight, dest_cell, lengths):
    groups = nx * nz
    rows = 2 * groups
    cells = 4 * groups
    ctx = kv_cache.shape[3]
    span = ctx // groups
    width = residual.shape[-1]
    bf = jnp.bfloat16
    f32 = jnp.float32
    dma = pltpu.SemaphoreType.DMA
    vmem = pl.BlockSpec(memory_space=pltpu.VMEM)
    hbm = pl.BlockSpec(memory_space=pltpu.HBM)
    handed, moved = pl.pallas_call(
        functools.partial(move_kernel, nx, nz, nt),
        out_shape=(pltpu.VMEM((1, 4, width), bf), pltpu.VMEM((1, 4, 2, ctx, HD), bf)),
        in_specs=[hbm] * 7,
        out_specs=(vmem, vmem),
        scratch_shapes=[
            pltpu.SMEM((rows,), jnp.int32),
            pltpu.SMEM((rows,), jnp.int32),
            pltpu.VMEM(queries.shape, bf),
            pltpu.VMEM(new_kv.shape, bf),
            pltpu.VMEM(residual.shape, bf),
            pltpu.VMEM((8, cells), jnp.int32),
            pltpu.SMEM((8, cells), jnp.int32),
            pltpu.VMEM((2, 2, ctx, HD), bf),
            pltpu.VMEM(out_weight.shape[1:], bf),
            pltpu.VMEM((rows + 1, span, HD), bf),
            pltpu.VMEM((rows + 1, span, HD), bf),
            pltpu.VMEM((cells, span, HD), bf),
            pltpu.VMEM((cells, span, HD), bf),
            pltpu.VMEM((nt, 2, width), f32),
            pltpu.VMEM((nt, 2, width), f32),
            pltpu.VMEM((2, width), bf),
            pltpu.VMEM((groups, 2, width), bf),
            dma((2,)), dma((5,)), dma, dma, dma((2,)), dma((4,)), dma, dma, dma, dma, dma, dma, dma, dma, dma, dma,
        ],
        compiler_params=pltpu.CompilerParams(
            collective_id=0, has_side_effects=True, vmem_limit_bytes=60 * 1024 * 1024
        ),
    )(dest_cell, lengths, queries, kv_cache, new_kv, residual, out_weight)
    return pl.pallas_call(
        write_kernel,
        out_shape=(
            jax.ShapeDtypeStruct(handed.shape, bf),
            jax.ShapeDtypeStruct(moved.shape, bf),
        ),
        in_specs=[vmem, vmem],
        out_specs=(hbm, hbm),
        scratch_shapes=[dma((9,))],
        compiler_params=pltpu.CompilerParams(vmem_limit_bytes=8 * 1024 * 1024),
    )(handed, moved)


def solution(mesh):
    in_specs = (
        P("section", "group", "tensor"),
        P("section", "group", None, None, "tensor"),
        P("section", "group", None, "tensor"),
        P("section", "group", "tensor"),
        P("section", "tensor", None),
        P(),
        P(),
    )
    out_specs = (P("section", "group", "tensor"), P("section", "group", None, None, "tensor"))
    nz = min(NZ, mesh.shape["group"] // 2)
    body = functools.partial(shards, mesh.shape["group"] // nz, nz, mesh.shape["tensor"])
    return jax.shard_map(body, mesh=mesh, in_specs=in_specs, out_specs=out_specs, check_vma=False)
```

```python
import functools

import jax
import jax.numpy as jnp
from jax import lax
from jax.experimental import pallas as pl
from jax.experimental.pallas import tpu as pltpu
from jax.sharding import PartitionSpec as P

HD = 128
NZ = 8
MESH = pl.DeviceIdType.MESH


def move_kernel(
    nx, nz, nt,
    dest_hbm, len_hbm, q_hbm, kv_hbm, fresh_hbm, res_hbm, w_hbm,
    handed_ref, cache_ref,
    dest_ref, len_ref, q_ref, fresh_ref, res_ref, row_of, row_of_ref,
    kv, w, got_k, got_v, put_k, put_v, part, red, lay_own, lay,
    in_sem, small_sem, row_sem, w_sem, own_sem, sent_sem, k1_sem, v1_sem, k2_sem, v2_sem, red_sent, red_sem, layz_sent, layx_sent, layz_sem, layx_sem,
):
    groups = nx * nz
    ctx = kv.shape[2]
    span = ctx // groups
    rows = 2 * groups
    g = lax.axis_index("group")
    s = lax.axis_index("section")
    t = lax.axis_index("tensor")
    x = lax.div(g, nz)
    z = lax.rem(g, nz)

    load_kv = [pltpu.make_async_copy(kv_hbm.at[0, :, c], kv.at[:, c], in_sem.at[c]) for c in range(2)]
    load_kv[0].start()
    small = [
        pltpu.make_async_copy(src, dst, small_sem.at[i])
        for i, (src, dst) in enumerate(
            ((len_hbm, len_ref), (fresh_hbm, fresh_ref), (q_hbm, q_ref), (dest_hbm, dest_ref), (res_hbm, res_ref))
        )
    ]
    load_len, load_fresh, *load_rest = small
    load_len.start()
    load_fresh.start()

    barrier = pltpu.get_barrier_semaphore()

    def greet_group(k, carry):
        pl.semaphore_signal(barrier, inc=1, device_id={"group": lax.rem(g + k, groups)}, device_id_type=MESH)
        return carry

    def greet_tensor(k, carry):
        pl.semaphore_signal(barrier, inc=1, device_id={"tensor": lax.rem(t + k, nt)}, device_id_type=MESH)
        return carry

    def greet_section(k, carry):
        pl.semaphore_signal(
            barrier, inc=1, device_id={"group": x * nz + lax.rem(z + k, nz), "section": 1 - s}, device_id_type=MESH
        )
        return carry

    lax.fori_loop(1, groups, greet_group, 0, unroll=True)
    lax.fori_loop(1, nt, greet_tensor, 0, unroll=True)
    lax.fori_loop(0, nz, greet_section, 0, unroll=True)

    for load in (load_kv[1], *load_rest):
        load.start()
    load_w = pltpu.make_async_copy(w_hbm.at[0], w, w_sem)
    load_w.start()

    load_len.wait()
    load_fresh.wait()
    len0 = len_ref[2 * g]
    len1 = len_ref[2 * g + 1]
    pos = lax.broadcasted_iota(jnp.int32, (ctx, HD), 0)
    mine = pl.ds(pl.multiple_of(span * g, span), span)

    def append(c, got):
        load_kv[c].wait()
        for r, n in ((0, len0), (1, len1)):
            token = jnp.broadcast_to(fresh_ref[0, r, c : c + 1, :].astype(jnp.float32), (ctx, HD))
            kv[r, c] = jnp.where(pos == n, token, kv[r, c].astype(jnp.float32)).astype(jnp.bfloat16)
            got[2 * g + r] = kv[r, c, mine, :]
        got[rows] = jnp.zeros((span, HD), jnp.bfloat16)

    append(0, got_k)
    pl.semaphore_wait(barrier, groups - 1 + nt - 1 + nz)

    z_offsets = [o for m in range(nz // 2 - 1, 0, -1) for o in (m, nz - m)]
    z_offsets[2:2] = [nz // 2]
    z_offsets.append(0)

    way = 1 - 2 * s

    later = z_offsets[nz // 2 :] + z_offsets[: nz // 2]
    z_partners = [lax.rem(z + jnp.where(s == 0, dz, nz - dz_later), nz) for dz, dz_later in zip(z_offsets, later)]

    def for_partners(low, high, send):
        def window(v, carry):
            for j in range(nz):
                d = lax.rem(x + way * (j + v) + nx * nz, nx) * nz + z_partners[j]
                if 0 in (z_offsets[j], later[j]):
                    pl.when(d != g)(functools.partial(send, d))
                else:
                    send(d)
            return carry

        lax.fori_loop(low, high, window, 0, unroll=True)

    def hop1(c, dst, sem, low, high):
        def send(d):
            pltpu.make_async_remote_copy(
                src_ref=kv.at[:, c, pl.ds(pl.multiple_of(span * d, span), span), :],
                dst_ref=dst.at[pl.ds(2 * g, 2)],
                send_sem=sent_sem.at[c],
                recv_sem=sem,
                device_id={"group": d},
                device_id_type=MESH,
            ).start()

        for_partners(low, high, send)

    hop1(0, got_k, k1_sem, 0, nx)
    append(1, got_v)
    hop1(1, got_v, v1_sem, 0, nx)

    for load in load_rest:
        load.wait()
    cells = row_of.shape[1]
    cell = lax.broadcasted_iota(jnp.int32, (8, cells), 1)

    def place(r, found):
        return jnp.where(cell == dest_ref[r], r, found)

    found = lax.fori_loop(0, rows, place, jnp.full((8, cells), rows, jnp.int32), unroll=8)
    row_of[...] = found
    load_row_of = pltpu.make_async_copy(row_of, row_of_ref, row_sem)
    load_row_of.start()

    qf = q_ref[0].astype(jnp.float32)
    q8 = jnp.concatenate(
        [qf[r : r + 1, h * HD : (h + 1) * HD] for r in range(2) for h in range(4)], axis=0
    ).astype(jnp.bfloat16)
    dims = (((1,), (1,)), ((), ()))
    first = lax.broadcasted_iota(jnp.int32, (8, ctx), 0) < 4
    scores = jnp.where(
        first,
        lax.dot_general(q8, kv[0, 0], dims, preferred_element_type=jnp.float32),
        lax.dot_general(q8, kv[1, 0], dims, preferred_element_type=jnp.float32),
    ) * (1.0 / HD**0.5)
    valid = lax.broadcasted_iota(jnp.int32, (8, ctx), 1) <= jnp.where(first, len0, len1)
    scores = jnp.where(valid, scores, -1e30)
    top = jnp.max(scores, axis=1, keepdims=True)
    e = jnp.where(valid, jnp.exp(scores - top), 0.0)
    weights = (e / jnp.sum(e, axis=1, keepdims=True)).astype(jnp.bfloat16)
    sub = lax.broadcasted_iota(jnp.int32, (8, HD), 0)
    attended = jnp.where(
        sub < 4,
        jnp.dot(weights, kv[0, 1], preferred_element_type=jnp.float32),
        jnp.dot(weights, kv[1, 1], preferred_element_type=jnp.float32),
    )
    lhs = jnp.concatenate(
        [jnp.where(sub % 4 == h, attended, 0.0) for h in range(4)], axis=1
    ).astype(jnp.bfloat16)

    def wait_bytes(ref, sem):
        pltpu.make_async_copy(ref, ref, sem).wait()

    def hop2(c, got, put, sem, low, high):
        def copy_slots(d):
            for slot in range(4):
                put[4 * d + slot] = got[row_of_ref[0, 4 * d + slot]]

        def send(d):
            copy_slots(d)
            pltpu.make_async_remote_copy(
                src_ref=put.at[pl.ds(4 * d, 4)],
                dst_ref=cache_ref.at[0, :, c, mine, :],
                send_sem=sent_sem.at[2 + c],
                recv_sem=sem,
                device_id={"group": d},
                device_id_type=MESH,
            ).start()

        for_partners(low, high, send)
        if high == nx:
            copy_slots(g)
            pltpu.make_async_copy(put.at[pl.ds(4 * g, 4)], cache_ref.at[0, :, c, mine, :], own_sem.at[c]).start()

    width = res_ref.shape[2]
    load_w.wait()

    def project(k, carry):
        d = lax.rem(t + k, nt)
        cols = pl.ds(pl.multiple_of(width * d, width), width)
        p8 = jnp.dot(lhs, w[:, cols], preferred_element_type=jnp.float32)
        both = jnp.concatenate(
            [jnp.sum(p8[0:4], axis=0, keepdims=True), jnp.sum(p8[4:8], axis=0, keepdims=True)], axis=0
        )
        part[d] = both

        @pl.when(k < nt)
        def _():
            pltpu.make_async_remote_copy(
                src_ref=part.at[d],
                dst_ref=red.at[t],
                send_sem=red_sent,
                recv_sem=red_sem,
                device_id={"tensor": d},
                device_id_type=MESH,
            ).start()

        return carry

    lax.fori_loop(1, nt + 1, project, 0)
    red[t] = part[t]

    load_row_of.wait()
    wait_bytes(got_k.at[pl.ds(0, rows - 2)], k1_sem)
    hop2(0, got_k, put_k, k2_sem, 0, nx)

    wait_bytes(red.at[pl.ds(0, nt - 1)], red_sem)
    total = red[0]
    for i in range(1, nt):
        total = total + red[i]
    total = total + res_ref[0].astype(jnp.float32)
    lay_own[...] = total.astype(jnp.bfloat16)

    def hand(k, carry):
        pltpu.make_async_remote_copy(
            src_ref=lay_own,
            dst_ref=lay.at[g],
            send_sem=layz_sent,
            recv_sem=layz_sem,
            device_id={"group": x * nz + lax.rem(z + k, nz), "section": 1 - s},
            device_id_type=MESH,
        ).start()
        return carry

    lax.fori_loop(0, nz, hand, 0, unroll=True)


    wait_bytes(got_v.at[pl.ds(0, rows - 2)], v1_sem)
    hop2(1, got_v, put_v, v2_sem, 0, nx // 2)

    ring = pl.ds(nz * x, nz)
    wait_bytes(lay.at[pl.ds(0, nz)], layz_sem)

    def spread(k, carry):
        pltpu.make_async_remote_copy(
            src_ref=lay.at[ring],
            dst_ref=lay.at[ring],
            send_sem=layx_sent,
            recv_sem=layx_sem,
            device_id={"group": lax.rem(x + k, nx) * nz + z},
            device_id_type=MESH,
        ).start()
        return carry

    lax.fori_loop(1, nx, spread, 0, unroll=True)

    hop2(1, got_v, put_v, v2_sem, nx // 2, nx)

    wait_bytes(lay.at[pl.ds(0, nz * (nx - 1))], layx_sem)
    out_rows = []
    for slot in range(4):
        r = row_of_ref[0, 4 * g + slot]
        both = lay[jnp.minimum(r, rows - 1) // 2].astype(jnp.float32)
        out_rows.append(jnp.where(r < rows, jnp.where(r % 2 == 0, both[0:1], both[1:2]), 0.0))
    handed_ref[0] = jnp.concatenate(out_rows, axis=0).astype(jnp.bfloat16)

    wait_bytes(part.at[pl.ds(0, nt - 1)], red_sent)
    wait_bytes(lay.at[pl.ds(0, nz)], layz_sent)
    wait_bytes(lay.at[pl.ds(0, nz * (nx - 1))], layx_sent)
    wait_bytes(got_k.at[pl.ds(0, rows - 2)], sent_sem.at[0])
    wait_bytes(got_v.at[pl.ds(0, rows - 2)], sent_sem.at[1])
    for c, put, sem in ((0, put_k, k2_sem), (1, put_v, v2_sem)):
        pltpu.make_async_copy(put.at[pl.ds(4 * g, 4)], cache_ref.at[0, :, c, mine, :], own_sem.at[c]).wait()
        wait_bytes(put.at[pl.ds(0, 4 * (groups - 1))], sent_sem.at[2 + c])
        wait_bytes(put.at[pl.ds(0, 4 * (groups - 1))], sem)


def write_kernel(handed, moved, handed_hbm, moved_hbm, sem):
    copies = [
        pltpu.make_async_copy(moved.at[0, i, c], moved_hbm.at[0, i, c], sem.at[2 * i + c])
        for i in range(4)
        for c in range(2)
    ]
    copies.append(pltpu.make_async_copy(handed, handed_hbm, sem.at[8]))
    for copy in copies:
        copy.start()
    for copy in copies:
        copy.wait()


def shards(nx, nz, nt, queries, kv_cache, new_kv, residual, out_weight, dest_cell, lengths):
    groups = nx * nz
    rows = 2 * groups
    cells = 4 * groups
    ctx = kv_cache.shape[3]
    span = ctx // groups
    width = residual.shape[-1]
    bf = jnp.bfloat16
    f32 = jnp.float32
    dma = pltpu.SemaphoreType.DMA
    vmem = pl.BlockSpec(memory_space=pltpu.VMEM)
    hbm = pl.BlockSpec(memory_space=pltpu.HBM)
    handed, moved = pl.pallas_call(
        functools.partial(move_kernel, nx, nz, nt),
        out_shape=(pltpu.VMEM((1, 4, width), bf), pltpu.VMEM((1, 4, 2, ctx, HD), bf)),
        in_specs=[hbm] * 7,
        out_specs=(vmem, vmem),
        scratch_shapes=[
            pltpu.SMEM((rows,), jnp.int32),
            pltpu.SMEM((rows,), jnp.int32),
            pltpu.VMEM(queries.shape, bf),
            pltpu.VMEM(new_kv.shape, bf),
            pltpu.VMEM(residual.shape, bf),
            pltpu.VMEM((8, cells), jnp.int32),
            pltpu.SMEM((8, cells), jnp.int32),
            pltpu.VMEM((2, 2, ctx, HD), bf),
            pltpu.VMEM(out_weight.shape[1:], bf),
            pltpu.VMEM((rows + 1, span, HD), bf),
            pltpu.VMEM((rows + 1, span, HD), bf),
            pltpu.VMEM((cells, span, HD), bf),
            pltpu.VMEM((cells, span, HD), bf),
            pltpu.VMEM((nt, 2, width), f32),
            pltpu.VMEM((nt, 2, width), f32),
            pltpu.VMEM((2, width), bf),
            pltpu.VMEM((groups, 2, width), bf),
            dma((2,)), dma((5,)), dma, dma, dma((2,)), dma((4,)), dma, dma, dma, dma, dma, dma, dma, dma, dma, dma,
        ],
        compiler_params=pltpu.CompilerParams(
            collective_id=0, has_side_effects=True, vmem_limit_bytes=60 * 1024 * 1024
        ),
    )(dest_cell, lengths, queries, kv_cache, new_kv, residual, out_weight)
    return pl.pallas_call(
        write_kernel,
        out_shape=(
            jax.ShapeDtypeStruct(handed.shape, bf),
            jax.ShapeDtypeStruct(moved.shape, bf),
        ),
        in_specs=[vmem, vmem],
        out_specs=(hbm, hbm),
        scratch_shapes=[dma((9,))],
        compiler_params=pltpu.CompilerParams(vmem_limit_bytes=8 * 1024 * 1024),
    )(handed, moved)


def solution(mesh):
    in_specs = (
        P("section", "group", "tensor"),
        P("section", "group", None, None, "tensor"),
        P("section", "group", None, "tensor"),
        P("section", "group", "tensor"),
        P("section", "tensor", None),
        P(),
        P(),
    )
    out_specs = (P("section", "group", "tensor"), P("section", "group", None, None, "tensor"))
    nz = min(NZ, mesh.shape["group"] // 2)
    body = functools.partial(shards, mesh.shape["group"] // nz, nz, mesh.shape["tensor"])
    return jax.shard_map(body, mesh=mesh, in_specs=in_specs, out_specs=out_specs, check_vma=False)
```
